256 devices in a mesh: dp: 16 (over x, z_hi, core), expert: 4 (over z_lo), mp: 4 (over y).
Axes of the slice: x: 4, y: 4, z: 8 (z_hi: 2, z_lo: 4; z = z_hi * 4 + z_lo), core: 2. Of those that a mesh axis runs over, the one named last changes fastest.
Arguments:
- hidden: bfloat16 [4, 8192, 6144], P('expert', 'dp', 'mp'), may hold values from -22 to 22
- out_grad: bfloat16 [4, 8192, 2080], P('expert', 'dp', 'mp'), may hold values from -1 to 1
- master: float32 [4, 6144, 2080], P('expert', ('mp', 'dp')), may hold values from -6 to 6
- row_prev: float32 [4, 6144], P('expert', ('mp', 'dp')), may hold values from 0.03 to 0.3
- col_prev: float32 [4, 2080], P('expert'), may hold values from 0.03 to 0.3
Outputs:
- params: bfloat16 [4, 6144, 2080], P('expert', 'mp')
- master_new: float32 [4, 6144, 2080], P('expert', ('mp', 'dp'))
- direction: float32 [4, 6144, 2080], P('expert', ('mp', 'dp'))
- row_stat: float32 [4, 6144], P('expert', ('mp', 'dp'))
- col_stat: float32 [4, 2080], P('expert')
The draws below stay inside these ranges and needn't reach their ends.
All inputs are finite; a program needn't handle non-finite values.
Results may differ from the reference program's by a relative error of at most 0.0004.
Values may be sent and summed in bfloat16 or wider, within the bound.
A program may use at most 128 MiB of HBM per device.

```python
import math
import jax
import jax.numpy as jnp
from jax import lax

D = 2080
FF = 6144
TOK_DEV = 512
STEP = 100
TOKENS = 8192
EXPERTS = 4


def feature_scales(key, experts, count):
    position = jnp.arange(count, dtype=jnp.float32) / count
    spread = jax.random.uniform(key, (experts, 1, count), jnp.float32)
    return jnp.power(3.0, position - 0.5) * jnp.power(10.0, spread - 0.5)


def draw_hidden(key, part):
    key = jax.random.fold_in(key, 11)
    scale_key, value_key = jax.random.split(key)
    scales = feature_scales(scale_key, EXPERTS, FF)
    values = jax.random.truncated_normal(value_key, -4.0, 4.0, (EXPERTS, TOKENS, FF), jnp.float32)
    return (values * scales).astype(jnp.bfloat16)


def draw_out_grad(key, part):
    key = jax.random.fold_in(key, 12)
    scale_key, value_key = jax.random.split(key)
    scales = feature_scales(scale_key, EXPERTS, D) / 22.0
    values = jax.random.truncated_normal(value_key, -4.0, 4.0, (EXPERTS, TOKENS, D), jnp.float32)
    return (values * scales).astype(jnp.bfloat16)


def levels(key, extent, cuts, least, largest):
    factor_of = 1.0
    for dim, blocks in cuts:
        draws = jax.random.uniform(jax.random.fold_in(jax.random.fold_in(key, 6), dim), (blocks,), jnp.float32, least / len(cuts), largest / len(cuts))
        factor_of = factor_of * jnp.repeat(jnp.exp(draws), extent[dim] // blocks).reshape((-1,) + (1,) * (len(extent) - 1 - dim))
    return factor_of


def normal_values(stream_key, extent, width, most, shards=(), kind=jnp.bfloat16):
    level = levels(stream_key, extent, shards, -0.22, 0.18) if shards else 1.0
    entries = jax.random.normal(stream_key, extent, jnp.float32) * width * level
    return jnp.minimum(jnp.maximum(entries, -most), most).astype(kind)


def setup_inputs(seed: int = 0) -> dict:
    splits = jax.random.split(jax.random.key(seed), 6)
    return {
        "hidden": draw_hidden(jax.random.fold_in(splits[5], 71), 0),
        "out_grad": draw_out_grad(jax.random.fold_in(splits[5], 71), 0),
        "master": normal_values(splits[2], (EXPERTS, FF, D), 1.0, 6.0, ((0, 4), (1, 64)), jnp.float32),
        "row_prev": jnp.clip(jnp.exp(math.log(0.3) - 2.3025852 * jax.random.uniform(splits[3], (EXPERTS, FF), jnp.float32) ** levels(splits[3], (EXPERTS, FF), ((0, 4), (1, 64)), -0.2, 0.2)), 0.03, 0.3),
        "col_prev": jnp.clip(jnp.exp(math.log(0.3) - 2.3025852 * jax.random.uniform(splits[4], (EXPERTS, D), jnp.float32) ** levels(splits[4], (EXPERTS, D), ((0, 4),), -0.2, 0.2)), 0.03, 0.3),
    }


DECAY_POWER = 0.8
EPS_GRAD = 1e-30
LEARNING_RATE = 0.01

def expert_step(inputs):
    hidden_one, grad_one, master_one, row_old, col_old = inputs
    decay_rate = 1.0 - STEP ** (-DECAY_POWER)
    hidden_blocks = hidden_one.reshape(TOKENS // TOK_DEV, TOK_DEV, FF)
    grad_blocks = grad_one.reshape(TOKENS // TOK_DEV, TOK_DEV, D)

    def add_block(running, block_pair):
        partial_value = jnp.dot(block_pair[0].T, block_pair[1], preferred_element_type=jnp.float32)
        return (running + partial_value, None)
    gradient, _ = lax.scan(add_block, jnp.zeros((FF, D), jnp.float32), (hidden_blocks, grad_blocks))
    squares = gradient * gradient + EPS_GRAD
    row_stat = decay_rate * row_old + (1.0 - decay_rate) * lax.optimization_barrier(jnp.mean(squares, axis=1))
    col_stat = decay_rate * col_old + (1.0 - decay_rate) * lax.optimization_barrier(jnp.mean(squares, axis=0))
    scaled = gradient / jnp.sqrt(row_stat[:, None] * col_stat[None, :])
    update_rms = jnp.sqrt(jnp.mean(scaled * scaled))
    direction = scaled / jnp.maximum(1.0, update_rms)
    master_new = master_one - LEARNING_RATE * direction
    return (master_new.astype(jnp.bfloat16), master_new, direction, row_stat, col_stat)

def reference(hidden, out_grad, master, row_prev, col_prev):
    params, master_new, direction, row_stat, col_stat = lax.map(expert_step, (hidden, out_grad, master, row_prev, col_prev))
    return (params, master_new, direction, row_stat, col_stat)
```

```python
import functools

import jax
import jax.numpy as jnp
from jax import lax
from jax.experimental import pallas as pl
from jax.experimental.pallas import tpu as pltpu
from jax.sharding import PartitionSpec as P

D = 2080
FF = 6144
STEP = 100
DECAY_POWER = 0.8
EPS_GRAD = 1e-30
LEARNING_RATE = 0.01

NX, NH, NC, NY = 4, 2, 2, 4
TOK = 512
ROWS = 96
SLOTS = NX * NH
WIDE = 512
BLOCK = D // NY
REST = BLOCK - WIDE
TAIL = 128
NB = NY + 1
PIECES = 3
PIECE = ROWS // PIECES
MESH = pl.DeviceIdType.MESH
F32 = jnp.float32
BF16 = jnp.bfloat16


def kernel(hidden_ref, grad_ref, master_ref, row_ref, col_ref,
           params_ref, new_ref, dir_ref, row_out, col_out,
           hid, turned, lhs, feats, tailf, wide_p, tail_p,
           got_a, got_b, got_c, got_z, tgot_a, tgot_b, tgot_c, tgot_z,
           gsum, tsum, nat, stat_a, stat_b, full,
           load_sem, copy_sem,
           ysend, yrecv, csend, crecv, hsend, hrecv,
           xsend, xrecv, zsend, zrecv, ssend, srecv,
           gsend, grecv, out_sem):
    dp, ex, y = lax.axis_index("dp"), lax.axis_index("expert"), lax.axis_index("mp")
    x, h, c = dp // 4, lax.rem(dp // 2, 2), lax.rem(dp, 2)
    step = 1 - 2 * c

    def dev(dx=0, dh=0, dc=0, dy=0):
        return (
            (lax.rem(x + dx + NX, NX) * NH + lax.rem(h + dh, NH)) * NC + lax.rem(c + dc, NC),
            ex,
            lax.rem(y + dy + NY, NY),
        )

    def remote(src, dst, send, recv, to):
        copy = pltpu.make_async_remote_copy(
            src_ref=src, dst_ref=dst, send_sem=send, recv_sem=recv,
            device_id=to, device_id_type=MESH)
        copy.start()
        return copy

    started = []

    load_h = pltpu.make_async_copy(hidden_ref, hid, load_sem.at[0])
    load_h.start()
    mine = pl.ds(pl.multiple_of(c * TOK, TOK), TOK)
    other = pl.ds(pl.multiple_of((1 - c) * TOK, TOK), TOK)
    load_g = pltpu.make_async_copy(grad_ref, feats.at[y, mine], load_sem.at[1])
    load_g.start()

    group_a = [(dx, dc) for dx in range(NX) for dc in range(NC) if (dx, dc) != (0, 0)]
    group_b = [(dy, dh) for dy in range(NY) for dh in range(NH) if (dy, dh) != (0, 0)]
    barrier = pltpu.get_barrier_semaphore()
    for dx, dc in group_a:
        pl.semaphore_signal(barrier, 1, device_id=dev(dx=dx, dc=dc), device_id_type=MESH)
    for dy, dh in group_b:
        pl.semaphore_signal(barrier, 1, device_id=dev(dy=dy, dh=dh), device_id_type=MESH)
    pl.semaphore_wait(barrier, len(group_a) + len(group_b))

    load_g.wait()
    own = feats.at[y, mine]
    up = remote(own, own, ysend.at[0], yrecv.at[2], dev(dy=1))
    down = remote(own, own, ysend.at[1], yrecv.at[1], dev(dy=-1))
    sib = remote(own, own, csend.at[0], crecv.at[0], dev(dc=1))
    started += [up, down, sib]

    load_h.wait()
    for g in range(4):
        part = hid[:, pl.ds(384 * g, 384)].T
        for q in range(4):
            turned[2 * g + q // 2, q % 2] = part[ROWS * q:ROWS * (q + 1), :]
    give = remote(turned.at[:, 1 - c], lhs.at[:, :, mine], hsend, hrecv, dev(dc=1))
    keep = pltpu.make_async_copy(turned.at[:, c], lhs.at[:, :, mine], copy_sem)
    keep.start()
    keep.wait()
    give.wait()

    wides = [wide_p.at[t] for t in range(NY)] + [tail_p]
    as_ = [got_a.at[t] for t in range(NY)] + [tgot_a]
    bs_ = [got_b.at[t] for t in range(NY)] + [tgot_b]
    cs_ = [got_c.at[t] for t in range(NY)] + [tgot_c]
    zs_ = [got_z.at[t] for t in range(NY)] + [tgot_z]
    offs = (0, 1, 3, 2)

    def chunk(t, dx):
        return wides[t].at[pl.ds(2 * lax.rem(x + dx + NX, NX), 2)]

    def product(t):
        left = lhs[...].reshape(SLOTS * ROWS, 2 * TOK)
        if t < NY:
            b = lax.rem(y + offs[t], NY)

            @pl.loop(0, WIDE // 256)
            def _(n):
                cols = pl.ds(pl.multiple_of(n * 256, 256), 256)
                wide_p[t, :, :, cols] = jnp.dot(
                    left, feats[b, :, cols], preferred_element_type=F32
                ).reshape(SLOTS, ROWS, 256)
        else:
            tail_p[...] = jnp.dot(
                left, tailf[...], preferred_element_type=F32
            ).reshape(SLOTS, ROWS, TAIL)
        started.append(remote(chunk(t, 2), as_[t], xsend.at[0, t], xrecv.at[0, t], dev(dx=step)))
        started.append(remote(chunk(t, -step), bs_[t], xsend.at[1, t], xrecv.at[1, t], dev(dx=-step)))

    def recv(dst, sem):
        pltpu.make_async_remote_copy(
            src_ref=dst, dst_ref=dst, send_sem=sem, recv_sem=sem,
            device_id=dev(dc=1), device_id_type=MESH).wait_recv()

    def forward_sum(t):
        recv(as_[t], xrecv.at[0, t])
        ref = chunk(t, step)
        ref[...] = ref[...] + as_[t][...]
        started.append(remote(ref, cs_[t], xsend.at[2, t], xrecv.at[2, t], dev(dx=step)))

    def own_sum(t):
        recv(bs_[t], xrecv.at[1, t])
        recv(cs_[t], xrecv.at[2, t])
        ref = chunk(t, 0)
        ref[...] = ref[...] + bs_[t][...] + cs_[t][...]
        started.append(remote(ref.at[1 - h], zs_[t], zsend.at[t], zrecv.at[t], dev(dh=1)))

    def finish(t):
        recv(zs_[t], zrecv.at[t])
        total = chunk(t, 0).at[h][...] + zs_[t][...]
        if t < NY:
            gsum[lax.rem(y + offs[t], NY)] = total
        else:
            tsum[...] = total

    def sib_forward(t):
        b = lax.rem(y + offs[t], NY)
        started.append(remote(feats.at[b, mine], feats.at[b, mine],
                              csend.at[t], crecv.at[t], dev(dc=1)))

    def block(t):
        b = lax.rem(y + offs[t], NY)
        return feats.at[b, mine], feats.at[b, other]

    recv(block(0)[1], crecv.at[0])
    product(0)
    forward_sum(0)
    recv(block(1)[0], yrecv.at[1])
    recv(block(2)[0], yrecv.at[2])
    on = feats.at[lax.rem(y - step + NY, NY), mine]
    started.append(remote(on, on, ysend.at[2], yrecv.at[3], dev(dy=step)))
    sib_forward(1)
    sib_forward(2)
    recv(block(1)[1], crecv.at[1])
    product(1)
    recv(block(2)[1], crecv.at[2])
    product(2)
    own_sum(0)
    forward_sum(1)
    recv(block(3)[0], yrecv.at[3])
    sib_forward(3)
    forward_sum(2)
    recv(block(3)[1], crecv.at[3])
    product(3)
    tailf[...] = jnp.zeros_like(tailf)
    for b in range(NY):
        tailf[:, REST * b:REST * (b + 1)] = feats[b, :, WIDE:BLOCK]
    product(4)
    own_sum(1)
    finish(0)
    forward_sum(3)
    forward_sum(4)
    own_sum(2)
    finish(1)
    own_sum(3)
    own_sum(4)
    finish(2)
    finish(3)
    finish(4)

    decay = 1.0 - STEP ** (-DECAY_POWER)
    for b in range(NY):
        nat[:, BLOCK * b:BLOCK * b + WIDE] = gsum[b]
        nat[:, BLOCK * b + WIDE:BLOCK * (b + 1)] = tsum[:, REST * b:REST * (b + 1)]
    squares = nat[...] * nat[...]
    row_mean = jnp.sum(squares + EPS_GRAD, axis=1, keepdims=True) / D
    eye = (lax.broadcasted_iota(jnp.int32, (ROWS, ROWS), 0)
           == lax.broadcasted_iota(jnp.int32, (ROWS, ROWS), 1))
    row_old = jnp.sum(jnp.where(eye, row_ref[...], 0.0), axis=1, keepdims=True)
    row_stat = decay * row_old + (1.0 - decay) * row_mean
    row_out[...] = jnp.sum(jnp.where(eye, row_stat, 0.0), axis=0, keepdims=True)
    slot_a = x * NC + c
    slot_b = y * NH + h
    stat_a[slot_a, 0:1] = jnp.sum(squares + EPS_GRAD, axis=0, keepdims=True)
    stat_a[slot_a, 1:2] = jnp.sum(squares / row_stat, axis=0, keepdims=True)
    for i, (dx, dc) in enumerate(group_a):
        started.append(remote(stat_a.at[slot_a], stat_a.at[slot_a], ssend.at[0, i], srecv.at[0, i],
                              dev(dx=dx, dc=dc)))
    for i, (dx, dc) in enumerate(group_a):
        recv(stat_a.at[lax.rem(x - dx + NX, NX) * NC + lax.rem(c + dc, NC)], srecv.at[0, i])
    stat_b[slot_b] = jnp.sum(stat_a[...], axis=0)
    for i, (dy, dh) in enumerate(group_b):
        started.append(remote(stat_b.at[slot_b], stat_b.at[slot_b], ssend.at[1, i], srecv.at[1, i],
                              dev(dy=dy, dh=dh)))
    for i, (dy, dh) in enumerate(group_b):
        recv(stat_b.at[lax.rem(y - dy + NY, NY) * NH + lax.rem(h + dh, NH)], srecv.at[1, i])
    sums = jnp.sum(stat_b[...], axis=0)
    col_stat = decay * col_ref[...] + (1.0 - decay) * (sums[0:1] / FF)
    col_out[...] = col_stat
    update_rms = jnp.sqrt(jnp.sum(sums[1:2] / col_stat, axis=1, keepdims=True) / (FF * D))
    scale = 1.0 / jnp.maximum(1.0, update_rms)
    direction = nat[...] * lax.rsqrt(row_stat) * (lax.rsqrt(col_stat) * scale)
    dir_ref[...] = direction
    master_new = master_ref[...] - LEARNING_RATE * direction
    new_ref[...] = master_new
    slot = x * NH + h
    full[slot, c] = master_new.astype(BF16)

    def piece(dx, dh, core, p):
        return full.at[lax.rem(x + dx + NX, NX) * NH + lax.rem(h + dh, NH), core, pl.ds(PIECE * p, PIECE)]

    outs = []

    def ready(ref_of, share, n):
        ref = ref_of
        if share is not None:
            started.append(remote(ref, ref, gsend.at[share], grecv.at[share], dev(dc=1)))
        del n

    def sem(kind, p):
        return kind * PIECES + p

    def send_along(kind, dh, dx, p, src_dx=0):
        ref = piece(src_dx, dh, c, p)
        started.append(remote(ref, ref, gsend.at[sem(kind, p)], grecv.at[sem(kind, p)], dev(dx=dx)))

    def share(kind, dx, dh, p):
        ref = piece(dx, dh, c, p)
        started.append(remote(ref, ref, gsend.at[sem(kind, p)], grecv.at[sem(kind, p)], dev(dc=1)))

    def got(kind, dx, dh, p, core):
        recv(piece(dx, dh, core, p), grecv.at[sem(kind, p)])

    for p in range(PIECES):
        ref = piece(0, 0, c, p)
        started.append(remote(ref, ref, gsend.at[sem(0, p)], grecv.at[sem(0, p)], dev(dh=1)))
        send_along(1, 0, 1, p)
        send_along(3, 0, -1, p)
    for p in range(PIECES):
        share(7, 0, 0, p)

    def pass_on(dh, p):
        kinds = (1, 3) if dh == 0 else (2, 4)
        got(kinds[0], -1, dh, p, c)
        got(kinds[1], 1, dh, p, c)
        send_along(5 + dh, dh, step, p, src_dx=-step)
        share(9 + dh, 1, dh, p)
        share(11 + dh, -1, dh, p)

    for p in range(PIECES):
        got(0, 0, 1, p, c)
        send_along(2, 1, 1, p)
        send_along(4, 1, -1, p)
        share(8, 0, 1, p)
        pass_on(0, p)
    for p in range(PIECES):
        pass_on(1, p)
        got(5, 2, 0, p, c)
        share(13, 2, 0, p)
    for p in range(PIECES):
        got(6, 2, 1, p, c)
        share(14, 2, 1, p)
    for p in range(PIECES):
        for dx in range(NX):
            pass
    for p in range(PIECES):
        got(7, 0, 0, p, 1 - c)
        got(8, 0, 1, p, 1 - c)
        for dh in range(NH):
            got(9 + dh, 1, dh, p, 1 - c)
            got(11 + dh, -1, dh, p, 1 - c)
            got(13 + dh, 2, dh, p, 1 - c)
    out = pltpu.make_async_copy(full, params_ref, out_sem)
    out.start()
    out.wait()
    for copy in started:
        copy.wait_send()


def local(hidden, out_grad, master, row_prev, col_prev):
    vmem = pl.BlockSpec(memory_space=pltpu.VMEM)
    anywhere = pl.BlockSpec(memory_space=pl.ANY)
    dma = pltpu.SemaphoreType.DMA
    params, master_new, direction, row_stat, col_stat = pl.pallas_call(
        kernel,
        out_shape=(
            jax.ShapeDtypeStruct((SLOTS, NC, ROWS, D), BF16),
            jax.ShapeDtypeStruct((ROWS, D), F32),
            jax.ShapeDtypeStruct((ROWS, D), F32),
            jax.ShapeDtypeStruct((1, ROWS), F32),
            jax.ShapeDtypeStruct((1, D), F32),
        ),
        in_specs=[anywhere, anywhere, vmem, vmem, vmem],
        out_specs=(anywhere, vmem, vmem, vmem, vmem),
        scratch_shapes=[
            pltpu.VMEM((TOK, NC * SLOTS * ROWS), BF16),
            pltpu.VMEM((SLOTS, NC, ROWS, TOK), BF16),
            pltpu.VMEM((SLOTS, ROWS, NC * TOK), BF16),
            pltpu.VMEM((NY, NC * TOK, BLOCK), BF16),
            pltpu.VMEM((NC * TOK, TAIL), BF16),
            pltpu.VMEM((NY, SLOTS, ROWS, WIDE), F32),
            pltpu.VMEM((SLOTS, ROWS, TAIL), F32),
            pltpu.VMEM((NY, NH, ROWS, WIDE), F32),
            pltpu.VMEM((NY, NH, ROWS, WIDE), F32),
            pltpu.VMEM((NY, NH, ROWS, WIDE), F32),
            pltpu.VMEM((NY, ROWS, WIDE), F32),
            pltpu.VMEM((NH, ROWS, TAIL), F32),
            pltpu.VMEM((NH, ROWS, TAIL), F32),
            pltpu.VMEM((NH, ROWS, TAIL), F32),
            pltpu.VMEM((ROWS, TAIL), F32),
            pltpu.VMEM((NY, ROWS, WIDE), F32),
            pltpu.VMEM((ROWS, TAIL), F32),
            pltpu.VMEM((ROWS, D), F32),
            pltpu.VMEM((NX * NC, 2, D), F32),
            pltpu.VMEM((NY * NH, 2, D), F32),
            pltpu.VMEM((SLOTS, NC, ROWS, D), BF16),
            dma((2,)), dma,
            dma((3,)), dma((4,)), dma((4,)), dma((4,)), dma, dma,
            dma((3, NB)), dma((3, NB)), dma((NB,)), dma((NB,)), dma((2, 7)), dma((2, 7)),
            dma((15 * PIECES,)), dma((15 * PIECES,)), dma,
        ],
        compiler_params=pltpu.CompilerParams(
            collective_id=0, has_side_effects=True, vmem_limit_bytes=60 * 2**20),
        cost_estimate=pl.CostEstimate(
            flops=2 * TOK * FF // NY * D, bytes_accessed=16 * 2**20, transcendentals=0),
        name="factored_step",
    )(hidden[0], out_grad[0], master[0], row_prev, col_prev)
    return (params.reshape(1, SLOTS * NC * ROWS, D), master_new[None], direction[None],
            row_stat, col_stat)


def solution(mesh):
    in_specs = (
        P("expert", "dp", "mp"),
        P("expert", "dp", "mp"),
        P("expert", ("mp", "dp"), None),
        P("expert", ("mp", "dp")),
        P("expert", None),
    )
    out_specs = (
        P("expert", "mp", None),
        P("expert", ("mp", "dp"), None),
        P("expert", ("mp", "dp"), None),
        P("expert", ("mp", "dp")),
        P("expert", None),
    )
    return jax.shard_map(local, mesh=mesh, in_specs=in_specs, out_specs=out_specs, check_vma=False)
```

```python
import functools

import jax
import jax.numpy as jnp
from jax import lax
from jax.experimental import pallas as pl
from jax.experimental.pallas import tpu as pltpu
from jax.sharding import PartitionSpec as P

D = 2080
FF = 6144
STEP = 100
DECAY_POWER = 0.8
EPS_GRAD = 1e-30
LEARNING_RATE = 0.01

NX, NH, NC, NY = 4, 2, 2, 4
TOK = 512
ROWS = 96
SLOTS = NX * NH
WIDE = 512
BLOCK = D // NY
REST = BLOCK - WIDE
HELD = WIDE + 16
TAIL = 128
NB = NY + 1
HALF = 1024
PART = 256
EXTRA = 128
PARTS = 5
MESH = pl.DeviceIdType.MESH
F32 = jnp.float32
BF16 = jnp.bfloat16

LEVELS = 21
REACH = 10.4 * 256
TINY = 1e-30


def split(value):
    high = value.astype(BF16)
    wide = high.astype(F32)
    inverse = pl.reciprocal(jnp.maximum(jnp.abs(wide), TINY), approx=True)
    return high, jnp.round((value - wide) * (inverse * REACH))


def encode(first, second, planes, rows):
    high_1, step_1 = split(first)
    high_2, step_2 = split(second)
    planes[0, rows] = high_1
    planes[1, rows] = high_2
    planes[2, rows] = (step_1 * LEVELS + step_2).astype(BF16)


def decode(planes, rows):
    low = planes[2, rows].astype(F32)
    step_1 = jnp.round(low * (1.0 / LEVELS))
    step_2 = low - LEVELS * step_1
    wide_1 = planes[0, rows].astype(F32)
    wide_2 = planes[1, rows].astype(F32)
    return (wide_1 + jnp.abs(wide_1) * (step_1 * (1.0 / REACH)),
            wide_2 + jnp.abs(wide_2) * (step_2 * (1.0 / REACH)))


def by_rows(count, body):
    @pl.loop(0, count // 16)
    def _(i):
        body(pl.multiple_of(i * 16, 16))


def kernel(hidden_ref, grad_ref, master_ref, row_ref, col_ref,
           params_ref, new_ref, dir_ref, row_out, col_out,
           hid, own_grad, turned, lhs, feats, tailf, wide_p, tail_p,
           out_x, out_z, tout_x, tout_z,
           got_x, got_z, tgot_x, tgot_z,
           gsum, tsum, nat, held_m, stat_a, stat_b, plain, rows_in,
           load_sem, copy_sem,
           ysend, yrecv, csend, crecv, hsend, hrecv,
           xsend, xrecv, zsend, zrecv, ssend, srecv,
           gsend, grecv):
    dp, ex, y = lax.axis_index("dp"), lax.axis_index("expert"), lax.axis_index("mp")
    x, h, c = dp // 4, lax.rem(dp // 2, 2), lax.rem(dp, 2)
    step = 1 - 2 * c

    def dev(dx=0, dh=0, dc=0, dy=0):
        return (
            (lax.rem(x + dx + NX, NX) * NH + lax.rem(h + dh, NH)) * NC + lax.rem(c + dc, NC),
            ex,
            lax.rem(y + dy + NY, NY),
        )

    def remote(src, dst, send, recv, to):
        copy = pltpu.make_async_remote_copy(
            src_ref=src, dst_ref=dst, send_sem=send, recv_sem=recv,
            device_id=to, device_id_type=MESH)
        copy.start()
        return copy

    started = []

    load_h = pltpu.make_async_copy(hidden_ref, hid, load_sem.at[0])
    load_h.start()
    mine = pl.ds(pl.multiple_of(c * TOK, TOK), TOK)
    other = pl.ds(pl.multiple_of((1 - c) * TOK, TOK), TOK)
    load_g = pltpu.make_async_copy(grad_ref, own_grad, load_sem.at[1])
    load_g.start()
    load_m = pltpu.make_async_copy(master_ref, held_m, load_sem.at[2])
    load_m.start()

    group_a = [(dx, dc) for dx in range(NX) for dc in range(NC) if (dx, dc) != (0, 0)]
    group_b = [(dy, dh) for dy in range(NY) for dh in range(NH) if (dy, dh) != (0, 0)]
    barrier = pltpu.get_barrier_semaphore()
    for dx, dc in group_a:
        pl.semaphore_signal(barrier, 1, device_id=dev(dx=dx, dc=dc), device_id_type=MESH)
    for dy, dh in group_b:
        pl.semaphore_signal(barrier, 1, device_id=dev(dy=dy, dh=dh), device_id_type=MESH)
    pl.semaphore_wait(barrier, len(group_a) + len(group_b))

    load_g.wait()
    feats[y, 0:WIDE, mine] = own_grad[0:WIDE, :]
    feats[y, WIDE:HELD, mine] = jnp.concatenate(
        [own_grad[WIDE:BLOCK, :], jnp.zeros((HELD - BLOCK, TOK), BF16)], axis=0)
    own = feats.at[y, :, mine]
    up = remote(own, own, ysend.at[0], yrecv.at[2], dev(dy=1))
    down = remote(own, own, ysend.at[1], yrecv.at[1], dev(dy=-1))
    sib = remote(own, own, csend.at[0], crecv.at[0], dev(dc=1))
    started += [up, down, sib]

    load_h.wait()
    for g in range(4):
        part = hid[:, pl.ds(384 * g, 384)].T
        for q in range(4):
            turned[2 * g + q // 2, q % 2] = part[ROWS * q:ROWS * (q + 1), :]
    give = remote(turned.at[:, 1 - c], lhs.at[:, :, mine], hsend.at[0], hrecv.at[0], dev(dc=1))
    keep = pltpu.make_async_copy(turned.at[:, c], lhs.at[:, :, mine], copy_sem)
    keep.start()
    keep.wait()
    give.wait()

    wides = [wide_p.at[t] for t in range(NY)] + [tail_p]
    offs = (0, 1, 3, 2)

    def sent_x(kind, t):
        return out_x.at[kind, t] if t < NY else tout_x.at[kind]

    def arrived_x(kind, t):
        return got_x.at[kind, t] if t < NY else tgot_x.at[kind]

    def chunk(t, dx):
        return wides[t].at[pl.ds(2 * lax.rem(x + dx + NX, NX), 2)]

    def send_x(kind, t, dx):
        started.append(remote(sent_x(kind, t), arrived_x(kind, t),
                              xsend.at[kind, t], xrecv.at[kind, t], dev(dx=dx)))

    def send_raw(kind, t, of, dx):
        ref, planes = chunk(t, of), sent_x(kind, t)

        def body(r):
            rows = pl.ds(r, 16)
            encode(ref[0, rows], ref[1, rows], planes, rows)

        by_rows(ROWS, body)
        send_x(kind, t, dx)

    def product(t):
        left = lhs[...].reshape(SLOTS * ROWS, 2 * TOK)
        if t < NY:
            b = lax.rem(y + offs[t], NY)

            @pl.loop(0, WIDE // 256)
            def _(n):
                cols = pl.ds(pl.multiple_of(n * 256, 256), 256)
                wide_p[t, :, :, cols] = lax.dot_general(
                    left, feats[b, cols, :], (((1,), (1,)), ((), ())),
                    preferred_element_type=F32).reshape(SLOTS, ROWS, 256)
        else:
            tail_p[...] = lax.dot_general(
                left, tailf[...], (((1,), (1,)), ((), ())),
                preferred_element_type=F32).reshape(SLOTS, ROWS, TAIL)
        send_raw(0, t, 2, step)
        send_raw(1, t, -step, -step)

    def recv(dst, sem):
        pltpu.make_async_remote_copy(
            src_ref=dst, dst_ref=dst, send_sem=sem, recv_sem=sem,
            device_id=dev(dc=1), device_id_type=MESH).wait_recv()

    def forward_sum(t):
        came, ref, planes = arrived_x(0, t), chunk(t, step), sent_x(2, t)
        recv(came, xrecv.at[0, t])

        def body(r):
            rows = pl.ds(r, 16)
            one, two = decode(came, rows)
            encode(ref[0, rows] + one, ref[1, rows] + two, planes, rows)

        by_rows(ROWS, body)
        send_x(2, t, step)

    def own_sum(t):
        ref, raw, summed = chunk(t, 0), arrived_x(1, t), arrived_x(2, t)
        planes, came = (out_z.at[t], got_z.at[t]) if t < NY else (tout_z, tgot_z)
        recv(raw, xrecv.at[1, t])
        recv(summed, xrecv.at[2, t])

        def body(r):
            rows = pl.ds(r, 16)
            one, two = decode(raw, rows)
            three, four = decode(summed, rows)
            ref[0, rows] = ref[0, rows] + one + three
            ref[1, rows] = ref[1, rows] + two + four

        by_rows(ROWS, body)
        given = ref.at[1 - h]

        def body_z(r):
            encode(given[pl.ds(r, 16)], given[pl.ds(r + ROWS // 2, 16)], planes, pl.ds(r, 16))

        by_rows(ROWS // 2, body_z)
        started.append(remote(planes, came, zsend.at[t], zrecv.at[t], dev(dh=1)))

    def finish(t):
        came = got_z.at[t] if t < NY else tgot_z
        dst = gsum.at[lax.rem(y + offs[t], NY)] if t < NY else tsum
        kept = chunk(t, 0).at[h]
        recv(came, zrecv.at[t])

        def body(r):
            one, two = decode(came, pl.ds(r, 16))
            dst[pl.ds(r, 16)] = kept[pl.ds(r, 16)] + one
            dst[pl.ds(r + ROWS // 2, 16)] = kept[pl.ds(r + ROWS // 2, 16)] + two

        by_rows(ROWS // 2, body)

    def sib_forward(t):
        b = lax.rem(y + offs[t], NY)
        started.append(remote(feats.at[b, :, mine], feats.at[b, :, mine],
                              csend.at[t], crecv.at[t], dev(dc=1)))

    def block(t):
        b = lax.rem(y + offs[t], NY)
        return feats.at[b, :, mine], feats.at[b, :, other]

    recv(block(0)[1], crecv.at[0])
    product(0)
    forward_sum(0)
    recv(block(1)[0], yrecv.at[1])
    recv(block(2)[0], yrecv.at[2])
    on = feats.at[lax.rem(y - step + NY, NY), :, mine]
    started.append(remote(on, on, ysend.at[2], yrecv.at[3], dev(dy=step)))
    sib_forward(1)
    sib_forward(2)
    recv(block(1)[1], crecv.at[1])
    product(1)
    recv(block(2)[1], crecv.at[2])
    product(2)
    own_sum(0)
    forward_sum(1)
    recv(block(3)[0], yrecv.at[3])
    sib_forward(3)
    forward_sum(2)
    recv(block(3)[1], crecv.at[3])
    product(3)
    tailf[...] = jnp.zeros_like(tailf)
    for b in range(NY):
        tailf[16 * b:16 * (b + 1)] = feats[b, WIDE:HELD]
    product(4)
    own_sum(1)
    finish(0)
    forward_sum(3)
    forward_sum(4)
    own_sum(2)
    finish(1)
    own_sum(3)
    own_sum(4)
    finish(2)
    finish(3)
    finish(4)

    decay = 1.0 - STEP ** (-DECAY_POWER)
    for b in range(NY):
        nat[:, BLOCK * b:BLOCK * b + WIDE] = gsum[b]
        nat[:, BLOCK * b + WIDE:BLOCK * (b + 1)] = tsum[:, 16 * b:16 * b + REST]
    squares = nat[...] * nat[...]
    row_mean = jnp.sum(squares + EPS_GRAD, axis=1, keepdims=True) / D
    eye = (lax.broadcasted_iota(jnp.int32, (ROWS, ROWS), 0)
           == lax.broadcasted_iota(jnp.int32, (ROWS, ROWS), 1))
    row_old = jnp.sum(jnp.where(eye, row_ref[...], 0.0), axis=1, keepdims=True)
    row_stat = decay * row_old + (1.0 - decay) * row_mean
    row_out[...] = jnp.sum(jnp.where(eye, row_stat, 0.0), axis=0, keepdims=True)
    slot_a = x * NC + c
    slot_b = y * NH + h
    stat_a[slot_a, 0:1] = jnp.sum(squares + EPS_GRAD, axis=0, keepdims=True)
    stat_a[slot_a, 1:2] = jnp.sum(squares / row_stat, axis=0, keepdims=True)
    for i, (dx, dc) in enumerate(group_a):
        started.append(remote(stat_a.at[slot_a], stat_a.at[slot_a], ssend.at[0, i], srecv.at[0, i],
                              dev(dx=dx, dc=dc)))
    for i, (dx, dc) in enumerate(group_a):
        recv(stat_a.at[lax.rem(x - dx + NX, NX) * NC + lax.rem(c + dc, NC)], srecv.at[0, i])
    stat_b[slot_b] = jnp.sum(stat_a[...], axis=0)
    for i, (dy, dh) in enumerate(group_b):
        started.append(remote(stat_b.at[slot_b], stat_b.at[slot_b], ssend.at[1, i], srecv.at[1, i],
                              dev(dy=dy, dh=dh)))
    for i, (dy, dh) in enumerate(group_b):
        recv(stat_b.at[lax.rem(y - dy + NY, NY) * NH + lax.rem(h + dh, NH)], srecv.at[1, i])
    sums = jnp.sum(stat_b[...], axis=0)
    load_m.wait()
    col_stat = decay * col_ref[...] + (1.0 - decay) * (sums[0:1] / FF)
    col_out[...] = col_stat
    update_rms = jnp.sqrt(jnp.sum(sums[1:2] / col_stat, axis=1, keepdims=True) / (FF * D))
    scale = 1.0 / jnp.maximum(1.0, update_rms)
    direction = nat[...] * lax.rsqrt(row_stat) * (lax.rsqrt(col_stat) * scale)
    dir_ref[...] = direction
    master_new = held_m[...] - LEARNING_RATE * direction
    new_ref[...] = master_new
    plain[:, 2048:2176] = jnp.zeros((ROWS, 128), BF16)
    plain[:, 0:D] = master_new.astype(BF16)

    rows_in[x, h, c] = plain[:, pl.ds(pl.multiple_of(c * HALF, HALF), HALF + EXTRA)]
    half = remote(plain.at[:, pl.ds(pl.multiple_of((1 - c) * HALF, HALF), HALF + EXTRA)],
                  rows_in.at[x, h, c], hsend.at[1], hrecv.at[1], dev(dc=1))
    half.wait()

    def each(p, body):
        if p < PARTS - 1:
            body()
        else:
            pl.when(c == 1)(body)

    def width(p):
        return (PART if p < PARTS - 1 else EXTRA)

    def piece(dx, dh, p):
        return rows_in.at[lax.rem(x + dx + NX, NX), lax.rem(h + dh, NH), :, :, pl.ds(PART * p, width(p))]

    waits = []
    back = -step

    def give_rows(kind, p, src_dx, dh, to):
        ref = piece(src_dx, dh, p)
        k = kind * PARTS + p
        pltpu.make_async_remote_copy(
            src_ref=ref, dst_ref=ref, send_sem=gsend.at[k], recv_sem=grecv.at[k],
            device_id=to, device_id_type=MESH).start()
        waits.append((p, k, lambda: piece(src_dx, dh, p)))

    def got(kind, dx, dh, p):
        recv(piece(dx, dh, p), grecv.at[kind * PARTS + p])

    def region(dx, p, core):
        size = PART if p < PARTS - 1 else D - 2 * HALF
        return (pl.ds(pl.multiple_of(core * HALF + PART * p, 32), size),
                pl.ds(pl.multiple_of(lax.rem(x + dx + NX, NX) * 384, 384), 384))

    def turn(i, dx, p):
        source = rows_in[lax.rem(x + dx + NX, NX), :, :, :, PART * p:PART * p + width(p)]
        value = source.reshape(NH * NC * ROWS, width(p)).T
        r, l = region(dx, p, c)
        params_ref[r, l] = value if p < PARTS - 1 else value[0:D - 2 * HALF]
        k = (7 + i) * PARTS + p
        ref = params_ref.at[r, l]
        pltpu.make_async_remote_copy(
            src_ref=ref, dst_ref=ref, send_sem=gsend.at[k], recv_sem=grecv.at[k],
            device_id=dev(dc=1), device_id_type=MESH).start()
        waits.append((p, k, lambda: params_ref.at[region(dx, p, c)]))

    for p in range(PARTS):
        def begin(p=p):
            give_rows(0, p, 0, 0, dev(dh=1))
            give_rows(1, p, 0, 0, dev(dx=1))
            give_rows(3, p, 0, 0, dev(dx=-1))
        each(p, begin)
    for p in range(PARTS):
        def middle(p=p):
            got(0, 0, 1, p)
            give_rows(2, p, 0, 1, dev(dx=1))
            give_rows(4, p, 0, 1, dev(dx=-1))
            turn(0, 0, p)
            got(1, -1, 0, p)
            got(3, 1, 0, p)
            give_rows(5, p, back, 0, dev(dx=step))
        each(p, middle)
    for p in range(PARTS):
        def late(p=p):
            got(2, -1, 1, p)
            got(4, 1, 1, p)
            give_rows(6, p, back, 1, dev(dx=step))
            turn(1, 1, p)
            turn(2, -1, p)
            got(5, 2, 0, p)
        each(p, late)
    for p in range(PARTS):
        def last(p=p):
            got(6, 2, 1, p)
            turn(3, 2, p)
        each(p, last)
    for p in range(PARTS):
        def shared(p=p):
            for i, dx in enumerate((0, 1, -1, 2)):
                r, l = region(dx, p, 1 - c)
                recv(params_ref.at[r, l], grecv.at[(7 + i) * PARTS + p])
        if p < PARTS - 1:
            shared()
        else:
            pl.when(c == 0)(shared)
    for p in range(PARTS):
        def sent(p=p):
            for q, k, of in waits:
                if q == p:
                    pltpu.make_async_remote_copy(
                        src_ref=of(), dst_ref=of(), send_sem=gsend.at[k], recv_sem=grecv.at[k],
                        device_id=dev(dc=1), device_id_type=MESH).wait_send()
        each(p, sent)
    for copy in started:
        copy.wait_send()


def local(hidden, out_grad, master, row_prev, col_prev):
    vmem = pl.BlockSpec(memory_space=pltpu.VMEM)
    anywhere = pl.BlockSpec(memory_space=pl.ANY)
    dma = pltpu.SemaphoreType.DMA
    params, master_new, direction, row_stat, col_stat = pl.pallas_call(
        kernel,
        out_shape=(
            pltpu.VMEM((D, NC * SLOTS * ROWS), BF16),
            pltpu.VMEM((ROWS, D), F32),
            pltpu.VMEM((ROWS, D), F32),
            pltpu.VMEM((1, ROWS), F32),
            pltpu.VMEM((1, D), F32),
        ),
        in_specs=[anywhere, anywhere, anywhere, vmem, vmem],
        out_specs=(vmem, vmem, vmem, vmem, vmem),
        scratch_shapes=[
            pltpu.VMEM((TOK, NC * SLOTS * ROWS), BF16),
            pltpu.VMEM((BLOCK, TOK), BF16),
            pltpu.VMEM((SLOTS, NC, ROWS, TOK), BF16),
            pltpu.VMEM((SLOTS, ROWS, NC * TOK), BF16),
            pltpu.VMEM((NY, HELD, NC * TOK), BF16),
            pltpu.VMEM((TAIL, NC * TOK), BF16),
            pltpu.VMEM((NY, SLOTS, ROWS, WIDE), F32),
            pltpu.VMEM((SLOTS, ROWS, TAIL), F32),
            pltpu.VMEM((3, NY, 3, ROWS, WIDE), BF16),
            pltpu.VMEM((NY, 3, ROWS // 2, WIDE), BF16),
            pltpu.VMEM((3, 3, ROWS, TAIL), BF16),
            pltpu.VMEM((3, ROWS // 2, TAIL), BF16),
            pltpu.VMEM((3, NY, 3, ROWS, WIDE), BF16),
            pltpu.VMEM((NY, 3, ROWS // 2, WIDE), BF16),
            pltpu.VMEM((3, 3, ROWS, TAIL), BF16),
            pltpu.VMEM((3, ROWS // 2, TAIL), BF16),
            pltpu.VMEM((NY, ROWS, WIDE), F32),
            pltpu.VMEM((ROWS, TAIL), F32),
            pltpu.VMEM((ROWS, D), F32),
            pltpu.VMEM((ROWS, D), F32),
            pltpu.VMEM((NX * NC, 2, D), F32),
            pltpu.VMEM((NY * NH, 2, D), F32),
            pltpu.VMEM((ROWS, HALF * 2 + EXTRA), BF16),
            pltpu.VMEM((NX, NH, NC, ROWS, HALF + EXTRA), BF16),
            dma((3,)), dma,
            dma((3,)), dma((4,)), dma((4,)), dma((4,)), dma((2,)), dma((2,)),
            dma((3, NB)), dma((3, NB)), dma((NB,)), dma((NB,)), dma((2, 7)), dma((2, 7)),
            dma((11 * PARTS,)), dma((11 * PARTS,)),
        ],
        compiler_params=pltpu.CompilerParams(
            collective_id=0, has_side_effects=True, vmem_limit_bytes=50 * 2**20),
        cost_estimate=pl.CostEstimate(
            flops=2 * TOK * FF // NY * D, bytes_accessed=16 * 2**20, transcendentals=0),
        name="factored_step",
    )(hidden[0], out_grad[0].T, master[0], row_prev, col_prev)
    return params.T[None], master_new[None], direction[None], row_stat, col_stat


def solution(mesh):
    in_specs = (
        P("expert", "dp", "mp"),
        P("expert", "dp", "mp"),
        P("expert", ("mp", "dp"), None),
        P("expert", ("mp", "dp")),
        P("expert", None),
    )
    out_specs = (
        P("expert", "mp", None),
        P("expert", ("mp", "dp"), None),
        P("expert", ("mp", "dp"), None),
        P("expert", ("mp", "dp")),
        P("expert", None),
    )
    return jax.shard_map(local, mesh=mesh, in_specs=in_specs, out_specs=out_specs, check_vma=False)
```

```python
import functools

import jax
import jax.numpy as jnp
from jax import lax
from jax.experimental import pallas as pl
from jax.experimental.pallas import tpu as pltpu
from jax.sharding import PartitionSpec as P

D = 2080
FF = 6144
STEP = 100
DECAY_POWER = 0.8
EPS_GRAD = 1e-30
LEARNING_RATE = 0.01

NX, NH, NC, NY = 4, 2, 2, 4
TOK = 512
ROWS = 96
SLOTS = NX * NH
WIDE = 512
BLOCK = D // NY
REST = BLOCK - WIDE
HELD = WIDE + 16
TAIL = 128
HALF = 1024
PART = 256
EXTRA = 128
PARTS = 5
MESH = pl.DeviceIdType.MESH
F32 = jnp.float32
BF16 = jnp.bfloat16

UNIT = 256
UNITS = NY * WIDE // UNIT

LEVELS = 21
REACH = 10.4 * 256
TINY = 1e-30


def last_place(wide):
    x = jnp.abs(wide) * 0.7515
    big = x * (2.0 ** 23 + 1.0)
    return big + (x - big)


def split(value, groups):
    high = value.astype(BF16)
    wide = high.astype(F32)
    if groups == 2:
        inverse = pl.reciprocal(jnp.maximum(jnp.abs(wide), TINY), approx=True)
        return high, jnp.round((value - wide) * (inverse * REACH))
    inverse = pl.reciprocal(jnp.maximum(last_place(wide), TINY), approx=True)
    step = jnp.floor((value - wide) * (inverse * 1024.0))
    return high, jnp.minimum(jnp.maximum(step, -4.0), 3.0)


def encode(values, planes, rows):
    groups = len(values)
    steps = []
    for i, value in enumerate(values):
        high, step = split(value, groups)
        planes[i, rows] = high
        steps.append(step)
    if groups == 2:
        low = steps[0] * LEVELS + steps[1]
    else:
        low = steps[0] * 64.0 + (steps[1] * 8.0 + (steps[2] + 36.0))
    planes[groups, rows] = low.astype(BF16)


def decode(groups, planes, rows):
    low = planes[groups, rows].astype(F32)
    wides = [planes[i, rows].astype(F32) for i in range(groups)]
    if groups == 2:
        step_1 = jnp.round(low * (1.0 / LEVELS))
        steps = (step_1, low - LEVELS * step_1)
        return [w + jnp.abs(w) * (q * (1.0 / REACH)) for w, q in zip(wides, steps)]
    step_1 = jnp.floor(low * (1.0 / 64))
    low = low - 64.0 * step_1
    step_2 = jnp.floor(low * (1.0 / 8))
    step_3 = low - 8.0 * step_2
    shifted = (step_1 + 0.5, step_2 - 3.5, step_3 - 3.5)
    return [w + last_place(w) * (q * (1.0 / 1024)) for w, q in zip(wides, shifted)]


GX, GZ = 3, 2
HALVES = (pl.ds(0, UNIT), pl.ds(UNIT, HELD - UNIT))
PAIR = NH * ROWS


def by_rows(count, body):
    @pl.loop(0, count // 16)
    def _(i):
        body(pl.multiple_of(i * 16, 16))


def kernel(hidden_ref, grad_ref, master_ref, row_ref, col_ref,
           params_ref, new_ref, dir_ref, row_out, col_out,
           hid, own_grad, turned, lhs, feats, tailf, wide_p, tail_p,
           out_x, out_z, tout_x, tout_z,
           got_x, got_z, tgot_x, tgot_z,
           gsum, tsum, nat, held_m, stat_a, stat_b, plain, rows_in,
           load_sem, copy_sem,
           ysend, yrecv, csend, crecv, hsend, hrecv,
           xsend, xrecv, zsend, zrecv, ssend, srecv,
           gsend, grecv, osend, orecv):
    dp, ex, y = lax.axis_index("dp"), lax.axis_index("expert"), lax.axis_index("mp")
    x, h, c = dp // 4, lax.rem(dp // 2, 2), lax.rem(dp, 2)
    step = 1 - 2 * c

    def dev(dx=0, dh=0, dc=0, dy=0):
        return (
            (lax.rem(x + dx + NX, NX) * NH + lax.rem(h + dh, NH)) * NC + lax.rem(c + dc, NC),
            ex,
            lax.rem(y + dy + NY, NY),
        )

    def remote(src, dst, send, recv, to):
        copy = pltpu.make_async_remote_copy(
            src_ref=src, dst_ref=dst, send_sem=send, recv_sem=recv,
            device_id=to, device_id_type=MESH)
        copy.start()
        return copy

    started = []

    load_h = pltpu.make_async_copy(hidden_ref, hid, load_sem.at[0])
    load_h.start()
    mine = pl.ds(pl.multiple_of(c * TOK, TOK), TOK)
    other = pl.ds(pl.multiple_of((1 - c) * TOK, TOK), TOK)
    load_g = pltpu.make_async_copy(grad_ref, own_grad, load_sem.at[1])
    load_g.start()
    load_m = pltpu.make_async_copy(master_ref, held_m, load_sem.at[2])
    load_m.start()

    group_a = [(dx, dc) for dx in range(NX) for dc in range(NC) if (dx, dc) != (0, 0)]
    group_b = [(dy, dh) for dy in range(NY) for dh in range(NH) if (dy, dh) != (0, 0)]
    barrier = pltpu.get_barrier_semaphore()
    for dx, dc in group_a:
        pl.semaphore_signal(barrier, 1, device_id=dev(dx=dx, dc=dc), device_id_type=MESH)
    for dy, dh in group_b:
        pl.semaphore_signal(barrier, 1, device_id=dev(dy=dy, dh=dh), device_id_type=MESH)

    load_h.wait()
    for g in range(4):
        part = hid[:, pl.ds(384 * g, 384)].T
        for q in range(4):
            turned[2 * g + q // 2, q % 2] = part[ROWS * q:ROWS * (q + 1), :]
    load_g.wait()
    feats[y, 0:WIDE, mine] = own_grad[0:WIDE, :]
    feats[y, WIDE:HELD, mine] = jnp.concatenate(
        [own_grad[WIDE:BLOCK, :], jnp.zeros((HELD - BLOCK, TOK), BF16)], axis=0)
    pl.semaphore_wait(barrier, len(group_a) + len(group_b))

    give_h = remote(turned.at[:, 1 - c], lhs.at[:, :, mine], hsend.at[0], hrecv.at[0], dev(dc=1))
    keep_h = pltpu.make_async_copy(turned.at[:, c], lhs.at[:, :, mine], copy_sem)
    keep_h.start()
    for i in range(2):
        own_i = feats.at[y, HALVES[i], mine]
        started.append(remote(own_i, own_i, csend.at[0, i], crecv.at[0, i], dev(dc=1)))
        started.append(remote(own_i, own_i, ysend.at[0, i], yrecv.at[2, i], dev(dy=1)))
        started.append(remote(own_i, own_i, ysend.at[1, i], yrecv.at[1, i], dev(dy=-1)))
    keep_h.wait()
    give_h.wait()

    offs = (0, 1, 3, 2)
    last = UNITS

    def sent_x(kind, u):
        return out_x.at[kind, u] if u < last else tout_x.at[kind]

    def arrived_x(kind, u):
        return got_x.at[kind, u] if u < last else tgot_x.at[kind]

    def chunk(u, dx):
        return (wide_p.at[u] if u < last else tail_p).at[lax.rem(x + dx + NX, NX)]

    def height(u):
        return PAIR if u < last else ROWS

    def times(left, right):
        return lax.dot_general(left, right, (((1,), (1,)), ((), ())), preferred_element_type=F32)

    def send_x(kind, u, dx):
        started.append(remote(sent_x(kind, u), arrived_x(kind, u),
                              xsend.at[kind, u], xrecv.at[kind, u], dev(dx=dx)))

    def spans(groups, total, r):
        return [pl.ds(i * (total // groups) + r, 16) for i in range(groups)]

    def send_raw(kind, u, of, dx):
        ref, planes = chunk(u, of), sent_x(kind, u)

        def body(r):
            encode([ref[rows] for rows in spans(GX, height(u), r)], planes, pl.ds(r, 16))

        by_rows(height(u) // GX, body)
        send_x(kind, u, dx)

    def product(u):
        if u < last:
            block, first = lax.rem(y + offs[u // 2], NY), UNIT * (u % 2)

        @pl.loop(0, NX)
        def _(i):
            if u < last:
                left = lhs[pl.ds(2 * i, 2)].reshape(PAIR, 2 * TOK)
                wide_p[u, i] = times(left, feats[block, first:first + UNIT, :])
            else:
                tail_p[i] = times(lhs[2 * i], tailf[0]) + times(lhs[2 * i + 1], tailf[1])

        send_raw(0, u, 2, step)
        send_raw(1, u, -step, -step)

    def recv(dst, sem):
        pltpu.make_async_remote_copy(
            src_ref=dst, dst_ref=dst, send_sem=sem, recv_sem=sem,
            device_id=dev(dc=1), device_id_type=MESH).wait_recv()

    def forward_sum(u):
        came, ref, planes = arrived_x(0, u), chunk(u, step), sent_x(2, u)
        recv(came, xrecv.at[0, u])

        def body(r):
            rows = pl.ds(r, 16)
            more = decode(GX, came, rows)
            encode([ref[at] + m for at, m in zip(spans(GX, height(u), r), more)], planes, rows)

        by_rows(height(u) // GX, body)
        send_x(2, u, step)

    def own_sum(u):
        ref, raw, summed = chunk(u, 0), arrived_x(1, u), arrived_x(2, u)
        planes, came = (out_z.at[u], got_z.at[u]) if u < last else (tout_z, tgot_z)
        recv(raw, xrecv.at[1, u])
        recv(summed, xrecv.at[2, u])

        def body(r):
            rows = pl.ds(r, 16)
            one, two = decode(GX, raw, rows), decode(GX, summed, rows)
            for at, m, n in zip(spans(GX, height(u), r), one, two):
                ref[at] = ref[at] + m + n

        by_rows(height(u) // GX, body)
        given = ref.at[pl.ds(pl.multiple_of((1 - h) * ROWS, ROWS), ROWS)] if u < last else ref

        def body_z(r):
            encode([given[at] for at in spans(GZ, ROWS, r)], planes, pl.ds(r, 16))

        by_rows(ROWS // GZ, body_z)
        started.append(remote(planes, came, zsend.at[u], zrecv.at[u], dev(dh=1)))

    def finish(u):
        came = got_z.at[u] if u < last else tgot_z
        dst = gsum.at[lax.rem(y + offs[u // 2], NY), u % 2] if u < last else tsum
        kept = chunk(u, 0)
        if u < last:
            kept = kept.at[pl.ds(pl.multiple_of(h * ROWS, ROWS), ROWS)]
        recv(came, zrecv.at[u])

        def body(r):
            for at, m in zip(spans(GZ, ROWS, r), decode(GZ, came, pl.ds(r, 16))):
                dst[at] = kept[at] + m

        by_rows(ROWS // GZ, body)

    def half_block(t, i, tokens):
        return feats.at[lax.rem(y + offs[t], NY), HALVES[i], tokens]

    def to_sibling(t, i):
        ref = half_block(t, i, mine)
        started.append(remote(ref, ref, csend.at[t, i], crecv.at[t, i], dev(dc=1)))

    def neighbours(i):
        recv(half_block(1, i, mine), yrecv.at[1, i])
        recv(half_block(2, i, mine), yrecv.at[2, i])
        on = feats.at[lax.rem(y - step + NY, NY), HALVES[i], mine]
        started.append(remote(on, on, ysend.at[2, i], yrecv.at[3, i], dev(dy=step)))
        to_sibling(1, i)
        to_sibling(2, i)

    def opposite(i):
        recv(half_block(3, i, mine), yrecv.at[3, i])
        to_sibling(3, i)

    def compute(t, i):
        recv(half_block(t, i, other), crecv.at[t, i])
        product(2 * t + i)

    def tail():
        tailf[...] = jnp.zeros_like(tailf)
        for b in range(NY):
            tailf[0, 16 * b:16 * (b + 1)] = feats[b, WIDE:HELD]
            tailf[1, 64 + 16 * b:64 + 16 * (b + 1)] = feats[b, WIDE:HELD]
        product(last)

    compute(0, 0)
    compute(0, 1)
    forward_sum(0)
    neighbours(0)
    compute(1, 0)
    compute(2, 0)
    forward_sum(1)
    own_sum(0)
    neighbours(1)
    compute(1, 1)
    compute(2, 1)
    forward_sum(2)
    opposite(0)
    compute(3, 0)
    own_sum(1)
    forward_sum(4)
    opposite(1)
    compute(3, 1)
    tail()
    forward_sum(3)
    own_sum(2)
    forward_sum(5)
    finish(0)
    own_sum(4)
    forward_sum(6)
    finish(1)
    own_sum(3)
    forward_sum(7)
    forward_sum(8)
    own_sum(5)
    finish(2)
    own_sum(6)
    finish(4)
    finish(3)
    own_sum(7)
    own_sum(8)
    finish(5)
    finish(6)
    finish(7)
    finish(8)

    decay = 1.0 - STEP ** (-DECAY_POWER)
    ends = jnp.where(h == 0, tsum[:, 0:64], tsum[:, 64:128])
    for b in range(NY):
        for i in range(2):
            nat[:, BLOCK * b + UNIT * i:BLOCK * b + UNIT * (i + 1)] = gsum[b, i]
        nat[:, BLOCK * b + WIDE:BLOCK * (b + 1)] = ends[:, 16 * b:16 * b + REST]
    squares = nat[...] * nat[...]
    row_mean = jnp.sum(squares + EPS_GRAD, axis=1, keepdims=True) / D
    eye = (lax.broadcasted_iota(jnp.int32, (ROWS, ROWS), 0)
           == lax.broadcasted_iota(jnp.int32, (ROWS, ROWS), 1))
    row_old = jnp.sum(jnp.where(eye, row_ref[...], 0.0), axis=1, keepdims=True)
    row_stat = decay * row_old + (1.0 - decay) * row_mean
    row_out[...] = jnp.sum(jnp.where(eye, row_stat, 0.0), axis=0, keepdims=True)
    slot_a = x * NC + c
    slot_b = y * NH + h
    stat_a[slot_a, 0:1] = jnp.sum(squares + EPS_GRAD, axis=0, keepdims=True)
    stat_a[slot_a, 1:2] = jnp.sum(squares / row_stat, axis=0, keepdims=True)
    for i, (dx, dc) in enumerate(group_a):
        started.append(remote(stat_a.at[slot_a], stat_a.at[slot_a], ssend.at[0, i], srecv.at[0, i],
                              dev(dx=dx, dc=dc)))
    for i, (dx, dc) in enumerate(group_a):
        recv(stat_a.at[lax.rem(x - dx + NX, NX) * NC + lax.rem(c + dc, NC)], srecv.at[0, i])
    stat_b[slot_b] = jnp.sum(stat_a[...], axis=0)
    for i, (dy, dh) in enumerate(group_b):
        started.append(remote(stat_b.at[slot_b], stat_b.at[slot_b], ssend.at[1, i], srecv.at[1, i],
                              dev(dy=dy, dh=dh)))
    for i, (dy, dh) in enumerate(group_b):
        recv(stat_b.at[lax.rem(y - dy + NY, NY) * NH + lax.rem(h + dh, NH)], srecv.at[1, i])
    sums = jnp.sum(stat_b[...], axis=0)
    load_m.wait()
    col_stat = decay * col_ref[...] + (1.0 - decay) * (sums[0:1] / FF)
    col_out[...] = col_stat
    update_rms = jnp.sqrt(jnp.sum(sums[1:2] / col_stat, axis=1, keepdims=True) / (FF * D))
    scale = 1.0 / jnp.maximum(1.0, update_rms)
    direction = nat[...] * lax.rsqrt(row_stat) * (lax.rsqrt(col_stat) * scale)
    dir_ref[...] = direction
    master_new = held_m[...] - LEARNING_RATE * direction
    new_ref[...] = master_new
    plain[:, 2048:2176] = jnp.zeros((ROWS, 128), BF16)
    plain[:, 0:D] = master_new.astype(BF16)

    rows_in[x, h, c] = plain[:, pl.ds(pl.multiple_of(c * HALF, HALF), HALF + EXTRA)]

    def whole(body):
        @pl.loop(0, PARTS - 1)
        def _(p):
            body(p, PART)

    def rest(body):
        @pl.when(c == 1)
        def _():
            body(PARTS - 1, EXTRA)

    def start_of(p):
        return PART * p if isinstance(p, int) else pl.multiple_of(p * PART, PART)

    def piece(dx, dh, p, width):
        return rows_in.at[lax.rem(x + dx + NX, NX), lax.rem(h + dh, NH), :, :, pl.ds(start_of(p), width)]

    def region(dx, p, core, width):
        size = width if width == PART else D - 2 * HALF
        return params_ref.at[
            pl.ds(pl.multiple_of(core * HALF + p * PART, 256 if width == PART else 1024), size),
            pl.ds(pl.multiple_of(lax.rem(x + dx + NX, NX) * 384, 384), 384)]

    def give(ref, kind, p, to):
        pltpu.make_async_remote_copy(
            src_ref=ref, dst_ref=ref, send_sem=gsend.at[kind, p], recv_sem=grecv.at[kind, p],
            device_id=to, device_id_type=MESH).start()

    def got(ref, kind, p):
        recv(ref, grecv.at[kind, p])

    def given(ref, kind, p):
        pltpu.make_async_remote_copy(
            src_ref=ref, dst_ref=ref, send_sem=gsend.at[kind, p], recv_sem=grecv.at[kind, p],
            device_id=dev(dc=1), device_id_type=MESH).wait_send()

    def turn(i, dx, p, width):
        ref = region(dx, p, c, width)
        for j in range(0, width, 128):
            at = j + start_of(p)
            at = at if isinstance(p, int) else pl.multiple_of(at, 128)
            value = rows_in[lax.rem(x + dx + NX, NX), :, :, :, pl.ds(at, 128)].reshape(NH * NC * ROWS, 128).T
            if width == PART:
                ref[j:j + 128, :] = value
            else:
                ref[...] = value[0:D - 2 * HALF]
        give(ref, 7 + i, p, dev(dc=1))

    ways = [(kind, k, to) for kind, to in enumerate((dict(dh=1), dict(dx=1), dict(dx=-1), dict()))
            for k in range(2) if (to or k)]

    def own_rows(p, width, kind, k, to):
        core = c if k == 0 else 1 - c
        src = plain.at[:, pl.ds(pl.multiple_of(core * HALF + start_of(p), 128), width)]
        return pltpu.make_async_remote_copy(
            src_ref=src, dst_ref=rows_in.at[x, h, c, :, pl.ds(start_of(p), width)],
            send_sem=osend.at[kind, k, p], recv_sem=orecv.at[kind, c, p],
            device_id=dev(dc=k, **to), device_id_type=MESH)

    def got_own(p, width, kind, dx, dh, owner):
        recv(rows_in.at[lax.rem(x + dx + NX, NX), lax.rem(h + dh, NH), owner, :, pl.ds(start_of(p), width)],
             orecv.at[kind, owner, p])

    def begin(p, width):
        for kind, k, to in ways:
            own_rows(p, width, kind, k, to).start()

    def begun(p, width):
        for kind, k, to in ways:
            own_rows(p, width, kind, k, to).wait_send()

    def middle(p, width):
        for owner in range(NC):
            got_own(p, width, 0, 0, 1, owner)
        ref = piece(0, 1, p, width)
        give(ref, 2, p, dev(dx=1))
        give(ref, 4, p, dev(dx=-1))
        for owner in range(NC):
            got_own(p, width, 1, -1, 0, owner)
            got_own(p, width, 2, 1, 0, owner)
        give(piece(-step, 0, p, width), 5, p, dev(dx=step))
        got_own(p, width, 3, 0, 0, 1 - c)
        turn(0, 0, p, width)

    def late(p, width):
        got(piece(-1, 1, p, width), 2, p)
        got(piece(1, 1, p, width), 4, p)
        give(piece(-step, 1, p, width), 6, p, dev(dx=step))
        turn(1, 1, p, width)
        turn(2, -1, p, width)

    def final(p, width):
        got(piece(2, 0, p, width), 5, p)
        got(piece(2, 1, p, width), 6, p)
        turn(3, 2, p, width)

    def shared(p, width):
        for i, dx in enumerate((0, 1, -1, 2)):
            got(region(dx, p, 1 - c, width), 7 + i, p)

    def sent(p, width):
        for kind, dx, dh in ((2, 0, 1), (4, 0, 1), (5, -step, 0), (6, -step, 1)):
            given(piece(dx, dh, p, width), kind, p)
        for i, dx in enumerate((0, 1, -1, 2)):
            given(region(dx, p, c, width), 7 + i, p)

    def extra_begin(body):
        for k in range(2):
            @pl.when(c == 1 - k)
            def _():
                for kind, k_, to in ways:
                    if k_ == k:
                        body(own_rows(PARTS - 1, EXTRA, kind, k, to))

    extra_begin(lambda copy: copy.start())
    whole(begin)
    for body in (middle, late, final):
        rest(body)
        whole(body)
    whole(shared)
    pl.when(c == 0)(lambda: shared(PARTS - 1, EXTRA))
    whole(sent)
    rest(sent)
    whole(begun)
    extra_begin(lambda copy: copy.wait_send())
    for copy in started:
        copy.wait_send()


def write(*refs):
    sem = refs[-1]
    copies = [pltpu.make_async_copy(refs[i], refs[i + 5], sem.at[i]) for i in range(5)]
    for copy in copies:
        copy.start()
    for copy in copies:
        copy.wait()


def local(hidden, out_grad, master, row_prev, col_prev):
    vmem = pl.BlockSpec(memory_space=pltpu.VMEM)
    anywhere = pl.BlockSpec(memory_space=pl.ANY)
    dma = pltpu.SemaphoreType.DMA
    results = pl.pallas_call(
        kernel,
        out_shape=(
            pltpu.VMEM((D, NC * SLOTS * ROWS), BF16),
            pltpu.VMEM((ROWS, D), F32),
            pltpu.VMEM((ROWS, D), F32),
            pltpu.VMEM((1, ROWS), F32),
            pltpu.VMEM((1, D), F32),
        ),
        in_specs=[anywhere, anywhere, anywhere, vmem, vmem],
        out_specs=(vmem, vmem, vmem, vmem, vmem),
        scratch_shapes=[
            pltpu.VMEM((TOK, NC * SLOTS * ROWS), BF16),
            pltpu.VMEM((BLOCK, TOK), BF16),
            pltpu.VMEM((SLOTS, NC, ROWS, TOK), BF16),
            pltpu.VMEM((SLOTS, ROWS, NC * TOK), BF16),
            pltpu.VMEM((NY, HELD, NC * TOK), BF16),
            pltpu.VMEM((NH, TAIL, NC * TOK), BF16),
            pltpu.VMEM((UNITS, NX, PAIR, UNIT), F32),
            pltpu.VMEM((NX, ROWS, TAIL), F32),
            pltpu.VMEM((3, UNITS, GX + 1, PAIR // GX, UNIT), BF16),
            pltpu.VMEM((UNITS, GZ + 1, ROWS // GZ, UNIT), BF16),
            pltpu.VMEM((3, GX + 1, ROWS // GX, TAIL), BF16),
            pltpu.VMEM((GZ + 1, ROWS // GZ, TAIL), BF16),
            pltpu.VMEM((3, UNITS, GX + 1, PAIR // GX, UNIT), BF16),
            pltpu.VMEM((UNITS, GZ + 1, ROWS // GZ, UNIT), BF16),
            pltpu.VMEM((3, GX + 1, ROWS // GX, TAIL), BF16),
            pltpu.VMEM((GZ + 1, ROWS // GZ, TAIL), BF16),
            pltpu.VMEM((NY, 2, ROWS, UNIT), F32),
            pltpu.VMEM((ROWS, TAIL), F32),
            pltpu.VMEM((ROWS, D), F32),
            pltpu.VMEM((ROWS, D), F32),
            pltpu.VMEM((NX * NC, 2, D), F32),
            pltpu.VMEM((NY * NH, 2, D), F32),
            pltpu.VMEM((ROWS, HALF * 2 + EXTRA), BF16),
            pltpu.VMEM((NX, NH, NC, ROWS, HALF + EXTRA), BF16),
            dma((3,)), dma,
            dma((3, 2)), dma((4, 2)), dma((4, 2)), dma((4, 2)), dma((1,)), dma((1,)),
            dma((3, UNITS + 1)), dma((3, UNITS + 1)), dma((UNITS + 1,)), dma((UNITS + 1,)),
            dma((2, 7)), dma((2, 7)),
            dma((11, PARTS)), dma((11, PARTS)), dma((4, 2, PARTS)), dma((4, 2, PARTS)),
        ],
        compiler_params=pltpu.CompilerParams(
            collective_id=0, has_side_effects=True, vmem_limit_bytes=50 * 2**20),
        cost_estimate=pl.CostEstimate(
            flops=2 * TOK * FF // NY * D, bytes_accessed=16 * 2**20, transcendentals=0),
        name="factored_step",
    )(hidden[0], out_grad[0].T, master[0], row_prev, col_prev)
    params, master_new, direction, row_stat, col_stat = pl.pallas_call(
        write,
        out_shape=[pltpu.HBM(r.shape, r.dtype) for r in results],
        in_specs=[vmem] * 5,
        out_specs=[pl.BlockSpec(memory_space=pltpu.HBM)] * 5,
        scratch_shapes=[dma((5,))],
        compiler_params=pltpu.CompilerParams(vmem_limit_bytes=2 * 2**20),
        name="write_results",
    )(*[pltpu.with_memory_space_constraint(r, pltpu.VMEM) for r in results])
    return params.T[None], master_new[None], direction[None], row_stat, col_stat


def solution(mesh):
    in_specs = (
        P("expert", "dp", "mp"),
        P("expert", "dp", "mp"),
        P("expert", ("mp", "dp"), None),
        P("expert", ("mp", "dp")),
        P("expert", None),
    )
    out_specs = (
        P("expert", "mp", None),
        P("expert", ("mp", "dp"), None),
        P("expert", ("mp", "dp"), None),
        P("expert", ("mp", "dp")),
        P("expert", None),
    )
    return jax.shard_map(local, mesh=mesh, in_specs=in_specs, out_specs=out_specs, check_vma=False)
```

```python
import functools

import jax
import jax.numpy as jnp
from jax import lax
from jax.experimental import pallas as pl
from jax.experimental.pallas import tpu as pltpu
from jax.sharding import PartitionSpec as P

D = 2080
FF = 6144
STEP = 100
DECAY_POWER = 0.8
EPS_GRAD = 1e-30
LEARNING_RATE = 0.01

NX, NH, NC, NY = 4, 2, 2, 4
TOK = 512
ROWS = 96
SLOTS = NX * NH
WIDE = 512
BLOCK = D // NY
REST = BLOCK - WIDE
HELD = WIDE + 16
TAIL = 128
HALF = 1024
PART = 256
EXTRA = 128
PARTS = 5
MIXED = 1
MESH = pl.DeviceIdType.MESH
F32 = jnp.float32
BF16 = jnp.bfloat16

UNIT = 256
UNITS = NY * WIDE // UNIT

LEVELS = 21
REACH = 10.4 * 256
TINY = 1e-30


def last_place(wide):
    x = jnp.abs(wide) * 0.7515
    big = x * (2.0 ** 23 + 1.0)
    return big + (x - big)


def split(value, groups):
    high = value.astype(BF16)
    wide = high.astype(F32)
    if groups == 2:
        inverse = pl.reciprocal(jnp.maximum(jnp.abs(wide), TINY), approx=True)
        return high, jnp.round((value - wide) * (inverse * REACH))
    inverse = pl.reciprocal(jnp.maximum(last_place(wide), TINY), approx=True)
    step = jnp.floor((value - wide) * (inverse * 1024.0))
    return high, jnp.minimum(jnp.maximum(step, -4.0), 3.0)


def encode(values, planes, rows):
    groups = len(values)
    steps = []
    for i, value in enumerate(values):
        high, step = split(value, groups)
        planes[i, rows] = high
        steps.append(step)
    if groups == 2:
        low = steps[0] * LEVELS + steps[1]
    else:
        low = steps[0] * 64.0 + (steps[1] * 8.0 + (steps[2] + 36.0))
    planes[groups, rows] = low.astype(BF16)


def decode(groups, planes, rows):
    low = planes[groups, rows].astype(F32)
    wides = [planes[i, rows].astype(F32) for i in range(groups)]
    if groups == 2:
        step_1 = jnp.round(low * (1.0 / LEVELS))
        steps = (step_1, low - LEVELS * step_1)
        return [w + jnp.abs(w) * (q * (1.0 / REACH)) for w, q in zip(wides, steps)]
    step_1 = jnp.floor(low * (1.0 / 64))
    low = low - 64.0 * step_1
    step_2 = jnp.floor(low * (1.0 / 8))
    step_3 = low - 8.0 * step_2
    shifted = (step_1 + 0.5, step_2 - 3.5, step_3 - 3.5)
    return [w + last_place(w) * (q * (1.0 / 1024)) for w, q in zip(wides, shifted)]


GX, GZ = 3, 2
HALVES = (pl.ds(0, UNIT), pl.ds(UNIT, HELD - UNIT))
PAIR = NH * ROWS


def by_rows(count, body):
    @pl.loop(0, count // 16)
    def _(i):
        body(pl.multiple_of(i * 16, 16))


def kernel(hidden_ref, grad_ref, master_ref, row_ref, col_ref,
           params_ref, new_ref, dir_ref, row_out, col_out,
           hid, own_grad, turned, lhs, feats, tailf, wide_p, tail_p,
           out_x, out_z, tout_x, tout_z,
           got_x, got_z, tgot_x, tgot_z,
           gsum, tsum, nat, held_m, stat_a, stat_b, plain, rows_in,
           load_sem, copy_sem,
           ysend, yrecv, csend, crecv, hsend, hrecv,
           xsend, xrecv, zsend, zrecv, ssend, srecv,
           gsend, grecv, osend, orecv):
    dp, ex, y = lax.axis_index("dp"), lax.axis_index("expert"), lax.axis_index("mp")
    x, h, c = dp // 4, lax.rem(dp // 2, 2), lax.rem(dp, 2)
    step = 1 - 2 * c

    def dev(dx=0, dh=0, dc=0, dy=0):
        return (
            (lax.rem(x + dx + NX, NX) * NH + lax.rem(h + dh, NH)) * NC + lax.rem(c + dc, NC),
            ex,
            lax.rem(y + dy + NY, NY),
        )

    def remote(src, dst, send, recv, to):
        copy = pltpu.make_async_remote_copy(
            src_ref=src, dst_ref=dst, send_sem=send, recv_sem=recv,
            device_id=to, device_id_type=MESH)
        copy.start()
        return copy

    started = []

    load_h = pltpu.make_async_copy(hidden_ref, hid, load_sem.at[0])
    load_h.start()
    mine = pl.ds(pl.multiple_of(c * TOK, TOK), TOK)
    other = pl.ds(pl.multiple_of((1 - c) * TOK, TOK), TOK)
    load_g = pltpu.make_async_copy(grad_ref, own_grad, load_sem.at[1])
    load_g.start()
    load_m = pltpu.make_async_copy(master_ref, held_m, load_sem.at[2])
    load_m.start()

    group_a = [(dx, dc) for dx in range(NX) for dc in range(NC) if (dx, dc) != (0, 0)]
    group_b = [(dy, dh) for dy in range(NY) for dh in range(NH) if (dy, dh) != (0, 0)]
    barrier = pltpu.get_barrier_semaphore()
    for dx, dc in group_a:
        pl.semaphore_signal(barrier, 1, device_id=dev(dx=dx, dc=dc), device_id_type=MESH)
    for dy, dh in group_b:
        pl.semaphore_signal(barrier, 1, device_id=dev(dy=dy, dh=dh), device_id_type=MESH)

    load_h.wait()
    for g in range(4):
        part = hid[:, pl.ds(384 * g, 384)].T
        for q in range(4):
            turned[2 * g + q // 2, q % 2] = part[ROWS * q:ROWS * (q + 1), :]
    load_g.wait()
    feats[y, 0:WIDE, mine] = own_grad[0:WIDE, :]
    feats[y, WIDE:HELD, mine] = jnp.concatenate(
        [own_grad[WIDE:BLOCK, :], jnp.zeros((HELD - BLOCK, TOK), BF16)], axis=0)
    pl.semaphore_wait(barrier, len(group_a) + len(group_b))

    give_h = remote(turned.at[:, 1 - c], lhs.at[:, :, mine], hsend.at[0], hrecv.at[0], dev(dc=1))
    keep_h = pltpu.make_async_copy(turned.at[:, c], lhs.at[:, :, mine], copy_sem)
    keep_h.start()
    for i in range(2):
        own_i = feats.at[y, HALVES[i], mine]
        started.append(remote(own_i, own_i, csend.at[0, i], crecv.at[0, i], dev(dc=1)))
        started.append(remote(own_i, own_i, ysend.at[0, i], yrecv.at[2, i], dev(dy=1)))
        started.append(remote(own_i, own_i, ysend.at[1, i], yrecv.at[1, i], dev(dy=-1)))
    keep_h.wait()
    give_h.wait()

    offs = (0, 1, 3, 2)
    last = UNITS

    def sent_x(kind, u):
        return out_x.at[kind, u] if u < last else tout_x.at[kind]

    def arrived_x(kind, u):
        return got_x.at[kind, u] if u < last else tgot_x.at[kind]

    def chunk(u, dx):
        return (wide_p.at[u] if u < last else tail_p).at[lax.rem(x + dx + NX, NX)]

    def height(u):
        return PAIR if u < last else ROWS

    def times(left, right):
        return lax.dot_general(left, right, (((1,), (1,)), ((), ())), preferred_element_type=F32)

    def send_x(kind, u, dx):
        started.append(remote(sent_x(kind, u), arrived_x(kind, u),
                              xsend.at[kind, u], xrecv.at[kind, u], dev(dx=dx)))

    def spans(groups, total, r):
        return [pl.ds(i * (total // groups) + r, 16) for i in range(groups)]

    def send_raw(kind, u, of, dx):
        ref, planes = chunk(u, of), sent_x(kind, u)

        def body(r):
            encode([ref[rows] for rows in spans(GX, height(u), r)], planes, pl.ds(r, 16))

        by_rows(height(u) // GX, body)
        send_x(kind, u, dx)

    def product(u):
        if u < last:
            block, first = lax.rem(y + offs[u // 2], NY), UNIT * (u % 2)

        @pl.loop(0, NX)
        def _(i):
            if u < last:
                left = lhs[pl.ds(2 * i, 2)].reshape(PAIR, 2 * TOK)
                wide_p[u, i] = times(left, feats[block, first:first + UNIT, :])
            else:
                tail_p[i] = times(lhs[2 * i], tailf[0]) + times(lhs[2 * i + 1], tailf[1])

        send_raw(0, u, 2, step)
        send_raw(1, u, -step, -step)

    def recv(dst, sem):
        pltpu.make_async_remote_copy(
            src_ref=dst, dst_ref=dst, send_sem=sem, recv_sem=sem,
            device_id=dev(dc=1), device_id_type=MESH).wait_recv()

    def forward_sum(u):
        came, ref, planes = arrived_x(0, u), chunk(u, step), sent_x(2, u)
        recv(came, xrecv.at[0, u])

        def body(r):
            rows = pl.ds(r, 16)
            more = decode(GX, came, rows)
            encode([ref[at] + m for at, m in zip(spans(GX, height(u), r), more)], planes, rows)

        by_rows(height(u) // GX, body)
        send_x(2, u, step)

    def own_sum(u):
        ref, raw, summed = chunk(u, 0), arrived_x(1, u), arrived_x(2, u)
        planes, came = (out_z.at[u], got_z.at[u]) if u < last else (tout_z, tgot_z)
        recv(raw, xrecv.at[1, u])
        recv(summed, xrecv.at[2, u])

        def body(r):
            rows = pl.ds(r, 16)
            one, two = decode(GX, raw, rows), decode(GX, summed, rows)
            for at, m, n in zip(spans(GX, height(u), r), one, two):
                ref[at] = ref[at] + m + n

        by_rows(height(u) // GX, body)
        given = ref.at[pl.ds(pl.multiple_of((1 - h) * ROWS, ROWS), ROWS)] if u < last else ref

        def body_z(r):
            encode([given[at] for at in spans(GZ, ROWS, r)], planes, pl.ds(r, 16))

        by_rows(ROWS // GZ, body_z)
        started.append(remote(planes, came, zsend.at[u], zrecv.at[u], dev(dh=1)))

    def finish(u):
        came = got_z.at[u] if u < last else tgot_z
        dst = gsum.at[lax.rem(y + offs[u // 2], NY), u % 2] if u < last else tsum
        kept = chunk(u, 0)
        if u < last:
            kept = kept.at[pl.ds(pl.multiple_of(h * ROWS, ROWS), ROWS)]
        recv(came, zrecv.at[u])

        def body(r):
            for at, m in zip(spans(GZ, ROWS, r), decode(GZ, came, pl.ds(r, 16))):
                dst[at] = kept[at] + m

        by_rows(ROWS // GZ, body)

    def half_block(t, i, tokens):
        return feats.at[lax.rem(y + offs[t], NY), HALVES[i], tokens]

    def to_sibling(t, i):
        ref = half_block(t, i, mine)
        started.append(remote(ref, ref, csend.at[t, i], crecv.at[t, i], dev(dc=1)))

    def neighbours(i):
        recv(half_block(1, i, mine), yrecv.at[1, i])
        recv(half_block(2, i, mine), yrecv.at[2, i])
        on = feats.at[lax.rem(y - step + NY, NY), HALVES[i], mine]
        started.append(remote(on, on, ysend.at[2, i], yrecv.at[3, i], dev(dy=step)))
        to_sibling(1, i)
        to_sibling(2, i)

    def opposite(i):
        recv(half_block(3, i, mine), yrecv.at[3, i])
        to_sibling(3, i)

    def compute(t, i):
        recv(half_block(t, i, other), crecv.at[t, i])
        product(2 * t + i)

    def tail():
        tailf[...] = jnp.zeros_like(tailf)
        for b in range(NY):
            tailf[0, 16 * b:16 * (b + 1)] = feats[b, WIDE:HELD]
            tailf[1, 64 + 16 * b:64 + 16 * (b + 1)] = feats[b, WIDE:HELD]
        product(last)

    compute(0, 0)
    compute(0, 1)
    forward_sum(0)
    neighbours(0)
    compute(1, 0)
    compute(2, 0)
    forward_sum(1)
    own_sum(0)
    neighbours(1)
    compute(1, 1)
    compute(2, 1)
    forward_sum(2)
    opposite(0)
    compute(3, 0)
    own_sum(1)
    forward_sum(4)
    opposite(1)
    compute(3, 1)
    tail()
    forward_sum(3)
    own_sum(2)
    forward_sum(5)
    finish(0)
    own_sum(4)
    forward_sum(6)
    finish(1)
    own_sum(3)
    forward_sum(7)
    forward_sum(8)
    own_sum(5)
    finish(2)
    own_sum(6)
    finish(4)
    finish(3)
    own_sum(7)
    own_sum(8)
    finish(5)
    finish(6)
    finish(7)
    finish(8)

    decay = 1.0 - STEP ** (-DECAY_POWER)
    ends = jnp.where(h == 0, tsum[:, 0:64], tsum[:, 64:128])
    for b in range(NY):
        for i in range(2):
            nat[:, BLOCK * b + UNIT * i:BLOCK * b + UNIT * (i + 1)] = gsum[b, i]
        nat[:, BLOCK * b + WIDE:BLOCK * (b + 1)] = ends[:, 16 * b:16 * b + REST]
    squares = nat[...] * nat[...]
    row_mean = jnp.sum(squares + EPS_GRAD, axis=1, keepdims=True) / D
    eye = (lax.broadcasted_iota(jnp.int32, (ROWS, ROWS), 0)
           == lax.broadcasted_iota(jnp.int32, (ROWS, ROWS), 1))
    row_old = jnp.sum(jnp.where(eye, row_ref[...], 0.0), axis=1, keepdims=True)
    row_stat = decay * row_old + (1.0 - decay) * row_mean
    row_out[...] = jnp.sum(jnp.where(eye, row_stat, 0.0), axis=0, keepdims=True)
    slot_a = x * NC + c
    slot_b = y * NH + h
    stat_a[slot_a, 0:1] = jnp.sum(squares + EPS_GRAD, axis=0, keepdims=True)
    stat_a[slot_a, 1:2] = jnp.sum(squares / row_stat, axis=0, keepdims=True)
    for i, (dx, dc) in enumerate(group_a):
        started.append(remote(stat_a.at[slot_a], stat_a.at[slot_a], ssend.at[0, i], srecv.at[0, i],
                              dev(dx=dx, dc=dc)))
    for i, (dx, dc) in enumerate(group_a):
        recv(stat_a.at[lax.rem(x - dx + NX, NX) * NC + lax.rem(c + dc, NC)], srecv.at[0, i])
    stat_b[slot_b] = jnp.sum(stat_a[...], axis=0)
    for i, (dy, dh) in enumerate(group_b):
        started.append(remote(stat_b.at[slot_b], stat_b.at[slot_b], ssend.at[1, i], srecv.at[1, i],
                              dev(dy=dy, dh=dh)))
    for i, (dy, dh) in enumerate(group_b):
        recv(stat_b.at[lax.rem(y - dy + NY, NY) * NH + lax.rem(h + dh, NH)], srecv.at[1, i])
    sums = jnp.sum(stat_b[...], axis=0)
    load_m.wait()
    col_stat = decay * col_ref[...] + (1.0 - decay) * (sums[0:1] / FF)
    col_out[...] = col_stat
    update_rms = jnp.sqrt(jnp.sum(sums[1:2] / col_stat, axis=1, keepdims=True) / (FF * D))
    scale = 1.0 / jnp.maximum(1.0, update_rms)
    direction = nat[...] * lax.rsqrt(row_stat) * (lax.rsqrt(col_stat) * scale)
    dir_ref[...] = direction
    master_new = held_m[...] - LEARNING_RATE * direction
    new_ref[...] = master_new
    plain[:, 2048:2176] = jnp.zeros((ROWS, 128), BF16)
    plain[:, 0:D] = master_new.astype(BF16)

    rows_in[x, h, c] = plain[:, pl.ds(pl.multiple_of(c * HALF, HALF), HALF + EXTRA)]

    def whole(body):
        @pl.loop(0, PARTS - 1)
        def _(p):
            body(p, PART)

    def rest(body):
        @pl.when(c == 1)
        def _():
            body(PARTS - 1, EXTRA)

    def start_of(p):
        return PART * p if isinstance(p, int) else pl.multiple_of(p * PART, PART)

    def piece(dx, dh, p, width):
        return rows_in.at[lax.rem(x + dx + NX, NX), lax.rem(h + dh, NH), :, :, pl.ds(start_of(p), width)]

    def region(dx, p, core, width):
        size = width if width == PART else D - 2 * HALF
        return params_ref.at[
            pl.ds(pl.multiple_of(core * HALF + p * PART, 256 if width == PART else 1024), size),
            pl.ds(pl.multiple_of(lax.rem(x + dx + NX, NX) * 384, 384), 384)]

    def give(ref, kind, p, to):
        pltpu.make_async_remote_copy(
            src_ref=ref, dst_ref=ref, send_sem=gsend.at[kind, p], recv_sem=grecv.at[kind, p],
            device_id=to, device_id_type=MESH).start()

    def got(ref, kind, p):
        recv(ref, grecv.at[kind, p])

    def given(ref, kind, p):
        pltpu.make_async_remote_copy(
            src_ref=ref, dst_ref=ref, send_sem=gsend.at[kind, p], recv_sem=grecv.at[kind, p],
            device_id=dev(dc=1), device_id_type=MESH).wait_send()

    def turn(i, dx, p, width):
        ref = region(dx, p, c, width)
        for j in range(0, width, 128):
            at = j + start_of(p)
            at = at if isinstance(p, int) else pl.multiple_of(at, 128)
            value = rows_in[lax.rem(x + dx + NX, NX), :, :, :, pl.ds(at, 128)].reshape(NH * NC * ROWS, 128).T
            if width == PART:
                ref[j:j + 128, :] = value
            else:
                ref[...] = value[0:D - 2 * HALF]
        give(ref, 7 + i, p, dev(dc=1))

    ways = [(kind, k, to) for kind, to in enumerate((dict(dh=1), dict(dx=1), dict(dx=-1), dict()))
            for k in range(2) if (to or k)]

    def own_rows(p, width, kind, k, to):
        core = c if k == 0 else 1 - c
        src = plain.at[:, pl.ds(pl.multiple_of(core * HALF + start_of(p), 128), width)]
        return pltpu.make_async_remote_copy(
            src_ref=src, dst_ref=rows_in.at[x, h, c, :, pl.ds(start_of(p), width)],
            send_sem=osend.at[kind, k, p], recv_sem=orecv.at[kind, c, p],
            device_id=dev(dc=k, **to), device_id_type=MESH)

    def got_own(p, width, kind, dx, dh, owner):
        recv(rows_in.at[lax.rem(x + dx + NX, NX), lax.rem(h + dh, NH), owner, :, pl.ds(start_of(p), width)],
             orecv.at[kind, owner, p])

    def begin(p, width):
        for kind, k, to in ways:
            own_rows(p, width, kind, k, to).start()

    def begun(p, width):
        for kind, k, to in ways:
            own_rows(p, width, kind, k, to).wait_send()

    def middle(p, width):
        for owner in range(NC):
            got_own(p, width, 0, 0, 1, owner)
        ref = piece(0, 1, p, width)
        give(ref, 2, p, dev(dx=1))
        give(ref, 4, p, dev(dx=-1))
        for owner in range(NC):
            got_own(p, width, 1, -1, 0, owner)
            got_own(p, width, 2, 1, 0, owner)
        give(piece(-step, 0, p, width), 5, p, dev(dx=step))
        got_own(p, width, 3, 0, 0, 1 - c)
        turn(0, 0, p, width)

    def late(p, width):
        got(piece(-1, 1, p, width), 2, p)
        got(piece(1, 1, p, width), 4, p)

        def along_x():
            give(piece(-step, 1, p, width), 6, p, dev(dx=step))

        if width == PART:
            pl.when(p >= MIXED)(along_x)
        else:
            along_x()
        turn(1, 1, p, width)
        turn(2, -1, p, width)

    def final(p, width):
        def across():
            got(piece(2, 0, p, width), 5, p)

        if width == PART:
            pl.when(p >= MIXED)(across)
        else:
            across()
        got(piece(2, 1, p, width), 6, p)
        turn(3, 2, p, width)

    def shared(p, width):
        for i, dx in enumerate((0, 1, -1, 2)):
            got(region(dx, p, 1 - c, width), 7 + i, p)

    def sent(p, width):
        for kind, dx, dh in ((2, 0, 1), (4, 0, 1), (5, -step, 0), (6, -step, 1)):
            given(piece(dx, dh, p, width), kind, p)
        for i, dx in enumerate((0, 1, -1, 2)):
            given(region(dx, p, c, width), 7 + i, p)

    def extra_begin(body):
        for k in range(2):
            @pl.when(c == 1 - k)
            def _():
                for kind, k_, to in ways:
                    if k_ == k:
                        body(own_rows(PARTS - 1, EXTRA, kind, k, to))

    extra_begin(lambda copy: copy.start())
    whole(begin)
    rest(middle)
    whole(middle)
    for p in range(MIXED):
        got(piece(2, 0, p, PART), 5, p)
        give(piece(2, 0, p, PART), 6, p, dev(dh=1))
    for body in (late, final):
        rest(body)
        whole(body)
    whole(shared)
    pl.when(c == 0)(lambda: shared(PARTS - 1, EXTRA))
    whole(sent)
    rest(sent)
    whole(begun)
    extra_begin(lambda copy: copy.wait_send())
    for copy in started:
        copy.wait_send()


def write(*refs):
    sem = refs[-1]
    copies = [pltpu.make_async_copy(refs[i], refs[i + 5], sem.at[i]) for i in range(5)]
    for copy in copies:
        copy.start()
    for copy in copies:
        copy.wait()


def local(hidden, out_grad, master, row_prev, col_prev):
    vmem = pl.BlockSpec(memory_space=pltpu.VMEM)
    anywhere = pl.BlockSpec(memory_space=pl.ANY)
    dma = pltpu.SemaphoreType.DMA
    results = pl.pallas_call(
        kernel,
        out_shape=(
            pltpu.VMEM((D, NC * SLOTS * ROWS), BF16),
            pltpu.VMEM((ROWS, D), F32),
            pltpu.VMEM((ROWS, D), F32),
            pltpu.VMEM((1, ROWS), F32),
            pltpu.VMEM((1, D), F32),
        ),
        in_specs=[anywhere, anywhere, anywhere, vmem, vmem],
        out_specs=(vmem, vmem, vmem, vmem, vmem),
        scratch_shapes=[
            pltpu.VMEM((TOK, NC * SLOTS * ROWS), BF16),
            pltpu.VMEM((BLOCK, TOK), BF16),
            pltpu.VMEM((SLOTS, NC, ROWS, TOK), BF16),
            pltpu.VMEM((SLOTS, ROWS, NC * TOK), BF16),
            pltpu.VMEM((NY, HELD, NC * TOK), BF16),
            pltpu.VMEM((NH, TAIL, NC * TOK), BF16),
            pltpu.VMEM((UNITS, NX, PAIR, UNIT), F32),
            pltpu.VMEM((NX, ROWS, TAIL), F32),
            pltpu.VMEM((3, UNITS, GX + 1, PAIR // GX, UNIT), BF16),
            pltpu.VMEM((UNITS, GZ + 1, ROWS // GZ, UNIT), BF16),
            pltpu.VMEM((3, GX + 1, ROWS // GX, TAIL), BF16),
            pltpu.VMEM((GZ + 1, ROWS // GZ, TAIL), BF16),
            pltpu.VMEM((3, UNITS, GX + 1, PAIR // GX, UNIT), BF16),
            pltpu.VMEM((UNITS, GZ + 1, ROWS // GZ, UNIT), BF16),
            pltpu.VMEM((3, GX + 1, ROWS // GX, TAIL), BF16),
            pltpu.VMEM((GZ + 1, ROWS // GZ, TAIL), BF16),
            pltpu.VMEM((NY, 2, ROWS, UNIT), F32),
            pltpu.VMEM((ROWS, TAIL), F32),
            pltpu.VMEM((ROWS, D), F32),
            pltpu.VMEM((ROWS, D), F32),
            pltpu.VMEM((NX * NC, 2, D), F32),
            pltpu.VMEM((NY * NH, 2, D), F32),
            pltpu.VMEM((ROWS, HALF * 2 + EXTRA), BF16),
            pltpu.VMEM((NX, NH, NC, ROWS, HALF + EXTRA), BF16),
            dma((3,)), dma,
            dma((3, 2)), dma((4, 2)), dma((4, 2)), dma((4, 2)), dma((1,)), dma((1,)),
            dma((3, UNITS + 1)), dma((3, UNITS + 1)), dma((UNITS + 1,)), dma((UNITS + 1,)),
            dma((2, 7)), dma((2, 7)),
            dma((11, PARTS)), dma((11, PARTS)), dma((4, 2, PARTS)), dma((4, 2, PARTS)),
        ],
        compiler_params=pltpu.CompilerParams(
            collective_id=0, has_side_effects=True, vmem_limit_bytes=50 * 2**20),
        cost_estimate=pl.CostEstimate(
            flops=2 * TOK * FF // NY * D, bytes_accessed=16 * 2**20, transcendentals=0),
        name="factored_step",
    )(hidden[0], out_grad[0].T, master[0], row_prev, col_prev)
    params, master_new, direction, row_stat, col_stat = pl.pallas_call(
        write,
        out_shape=[pltpu.HBM(r.shape, r.dtype) for r in results],
        in_specs=[vmem] * 5,
        out_specs=[pl.BlockSpec(memory_space=pltpu.HBM)] * 5,
        scratch_shapes=[dma((5,))],
        compiler_params=pltpu.CompilerParams(vmem_limit_bytes=2 * 2**20),
        name="write_results",
    )(*[pltpu.with_memory_space_constraint(r, pltpu.VMEM) for r in results])
    return params.T[None], master_new[None], direction[None], row_stat, col_stat


def solution(mesh):
    in_specs = (
        P("expert", "dp", "mp"),
        P("expert", "dp", "mp"),
        P("expert", ("mp", "dp"), None),
        P("expert", ("mp", "dp")),
        P("expert", None),
    )
    out_specs = (
        P("expert", "mp", None),
        P("expert", ("mp", "dp"), None),
        P("expert", ("mp", "dp"), None),
        P("expert", ("mp", "dp")),
        P("expert", None),
    )
    return jax.shard_map(local, mesh=mesh, in_specs=in_specs, out_specs=out_specs, check_vma=False)
```

```python
import functools

import jax
import jax.numpy as jnp
from jax import lax
from jax.experimental import pallas as pl
from jax.experimental.pallas import tpu as pltpu
from jax.sharding import PartitionSpec as P

D = 2080
FF = 6144
STEP = 100
DECAY_POWER = 0.8
EPS_GRAD = 1e-30
LEARNING_RATE = 0.01

NX, NH, NC, NY = 4, 2, 2, 4
TOK = 512
ROWS = 96
SLOTS = NX * NH
WIDE = 512
BLOCK = D // NY
REST = BLOCK - WIDE
HELD = WIDE + 16
TAIL = 128
HALF = 1024
PART = 256
EXTRA = 128
OVER = D - 2 * HALF
PARTS = 5
MIXED = 1
MESH = pl.DeviceIdType.MESH
F32 = jnp.float32
BF16 = jnp.bfloat16

UNIT = 256
UNITS = NY * WIDE // UNIT

LEVELS = 21
REACH = 10.4 * 256
TINY = 1e-30


def last_place(wide):
    x = jnp.abs(wide) * 0.7515
    big = x * (2.0 ** 23 + 1.0)
    return big + (x - big)


def split(value, groups):
    high = value.astype(BF16)
    wide = high.astype(F32)
    if groups == 2:
        inverse = pl.reciprocal(jnp.maximum(jnp.abs(wide), TINY), approx=True)
        return high, jnp.round((value - wide) * (inverse * REACH))
    inverse = pl.reciprocal(jnp.maximum(last_place(wide), TINY), approx=True)
    step = jnp.floor((value - wide) * (inverse * 1024.0))
    return high, jnp.minimum(jnp.maximum(step, -4.0), 3.0)


def encode(values, planes, rows):
    groups = len(values)
    steps = []
    for i, value in enumerate(values):
        high, step = split(value, groups)
        planes[i, rows] = high
        steps.append(step)
    if groups == 2:
        low = steps[0] * LEVELS + steps[1]
    else:
        low = steps[0] * 64.0 + (steps[1] * 8.0 + (steps[2] + 36.0))
    planes[groups, rows] = low.astype(BF16)


def decode(groups, planes, rows):
    low = planes[groups, rows].astype(F32)
    wides = [planes[i, rows].astype(F32) for i in range(groups)]
    if groups == 2:
        step_1 = jnp.round(low * (1.0 / LEVELS))
        steps = (step_1, low - LEVELS * step_1)
        return [w + jnp.abs(w) * (q * (1.0 / REACH)) for w, q in zip(wides, steps)]
    step_1 = jnp.floor(low * (1.0 / 64))
    low = low - 64.0 * step_1
    step_2 = jnp.floor(low * (1.0 / 8))
    step_3 = low - 8.0 * step_2
    shifted = (step_1 + 0.5, step_2 - 3.5, step_3 - 3.5)
    return [w + last_place(w) * (q * (1.0 / 1024)) for w, q in zip(wides, shifted)]


GX, GZ = 3, 2
HALVES = (pl.ds(0, UNIT), pl.ds(UNIT, HELD - UNIT))
PAIR = NH * ROWS


def by_rows(count, body):
    @pl.loop(0, count // 16)
    def _(i):
        body(pl.multiple_of(i * 16, 16))


def kernel(hidden_ref, grad_ref, master_ref, row_ref, col_ref,
           params_ref, new_ref, dir_ref, row_out, col_out,
           hid, own_grad, turned, lhs, feats, tailf, wide_p, tail_p,
           out_x, out_z, tout_x, tout_z,
           got_x, got_z, tgot_x, tgot_z,
           gsum, tsum, nat, held_m, stat_a, stat_b, plain, rows_in, plain_e, rows_e, wide_e,
           load_sem, copy_sem,
           ysend, yrecv, csend, crecv, hsend, hrecv,
           xsend, xrecv, zsend, zrecv, ssend, srecv,
           gsend, grecv, osend, orecv):
    dp, ex, y = lax.axis_index("dp"), lax.axis_index("expert"), lax.axis_index("mp")
    x, h, c = dp // 4, lax.rem(dp // 2, 2), lax.rem(dp, 2)
    step = 1 - 2 * c

    def dev(dx=0, dh=0, dc=0, dy=0):
        return (
            (lax.rem(x + dx + NX, NX) * NH + lax.rem(h + dh, NH)) * NC + lax.rem(c + dc, NC),
            ex,
            lax.rem(y + dy + NY, NY),
        )

    def remote(src, dst, send, recv, to):
        copy = pltpu.make_async_remote_copy(
            src_ref=src, dst_ref=dst, send_sem=send, recv_sem=recv,
            device_id=to, device_id_type=MESH)
        copy.start()
        return copy

    started = []

    load_h = pltpu.make_async_copy(hidden_ref, hid, load_sem.at[0])
    load_h.start()
    mine = pl.ds(pl.multiple_of(c * TOK, TOK), TOK)
    other = pl.ds(pl.multiple_of((1 - c) * TOK, TOK), TOK)
    load_g = pltpu.make_async_copy(grad_ref, own_grad, load_sem.at[1])
    load_g.start()
    load_m = pltpu.make_async_copy(master_ref, held_m, load_sem.at[2])
    load_m.start()

    group_a = [(dx, dc) for dx in range(NX) for dc in range(NC) if (dx, dc) != (0, 0)]
    group_b = [(dy, dh) for dy in range(NY) for dh in range(NH) if (dy, dh) != (0, 0)]
    barrier = pltpu.get_barrier_semaphore()
    for dx, dc in group_a:
        pl.semaphore_signal(barrier, 1, device_id=dev(dx=dx, dc=dc), device_id_type=MESH)
    for dy, dh in group_b:
        pl.semaphore_signal(barrier, 1, device_id=dev(dy=dy, dh=dh), device_id_type=MESH)

    load_h.wait()
    for g in range(4):
        part = hid[:, pl.ds(384 * g, 384)].T
        for q in range(4):
            turned[2 * g + q // 2, q % 2] = part[ROWS * q:ROWS * (q + 1), :]
    load_g.wait()
    feats[y, 0:WIDE, mine] = own_grad[0:WIDE, :]
    feats[y, WIDE:HELD, mine] = jnp.concatenate(
        [own_grad[WIDE:BLOCK, :], jnp.zeros((HELD - BLOCK, TOK), BF16)], axis=0)
    pl.semaphore_wait(barrier, len(group_a) + len(group_b))

    give_h = remote(turned.at[:, 1 - c], lhs.at[:, :, mine], hsend.at[0], hrecv.at[0], dev(dc=1))
    keep_h = pltpu.make_async_copy(turned.at[:, c], lhs.at[:, :, mine], copy_sem)
    keep_h.start()
    for i in range(2):
        own_i = feats.at[y, HALVES[i], mine]
        started.append(remote(own_i, own_i, csend.at[0, i], crecv.at[0, i], dev(dc=1)))
        started.append(remote(own_i, own_i, ysend.at[0, i], yrecv.at[2, i], dev(dy=1)))
        started.append(remote(own_i, own_i, ysend.at[1, i], yrecv.at[1, i], dev(dy=-1)))
    keep_h.wait()
    give_h.wait()

    offs = (0, 1, 3, 2)
    last = UNITS

    def sent_x(kind, u):
        return out_x.at[kind, u] if u < last else tout_x.at[kind]

    def arrived_x(kind, u):
        return got_x.at[kind, u] if u < last else tgot_x.at[kind]

    def chunk(u, dx):
        return (wide_p.at[u] if u < last else tail_p).at[lax.rem(x + dx + NX, NX)]

    def height(u):
        return PAIR if u < last else ROWS

    def times(left, right):
        return lax.dot_general(left, right, (((1,), (1,)), ((), ())), preferred_element_type=F32)

    def send_x(kind, u, dx):
        started.append(remote(sent_x(kind, u), arrived_x(kind, u),
                              xsend.at[kind, u], xrecv.at[kind, u], dev(dx=dx)))

    def spans(groups, total, r):
        return [pl.ds(i * (total // groups) + r, 16) for i in range(groups)]

    def send_raw(kind, u, of, dx):
        ref, planes = chunk(u, of), sent_x(kind, u)

        def body(r):
            encode([ref[rows] for rows in spans(GX, height(u), r)], planes, pl.ds(r, 16))

        by_rows(height(u) // GX, body)
        send_x(kind, u, dx)

    def product(u):
        if u < last:
            block, first = lax.rem(y + offs[u // 2], NY), UNIT * (u % 2)

        @pl.loop(0, NX // 2)
        def _(i):
            if u < last:
                left = lhs[pl.ds(4 * i, 4)].reshape(2 * PAIR, 2 * TOK)
                wide_p[u, pl.ds(2 * i, 2)] = times(
                    left, feats[block, first:first + UNIT, :]).reshape(2, PAIR, UNIT)
            else:
                for j in range(2):
                    at = 2 * i + j
                    tail_p[at] = times(lhs[2 * at], tailf[0]) + times(lhs[2 * at + 1], tailf[1])

        send_raw(0, u, 2, step)
        send_raw(1, u, -step, -step)

    def recv(dst, sem):
        pltpu.make_async_remote_copy(
            src_ref=dst, dst_ref=dst, send_sem=sem, recv_sem=sem,
            device_id=dev(dc=1), device_id_type=MESH).wait_recv()

    def forward_sum(u):
        came, ref, planes = arrived_x(0, u), chunk(u, step), sent_x(2, u)
        recv(came, xrecv.at[0, u])

        def body(r):
            rows = pl.ds(r, 16)
            more = decode(GX, came, rows)
            encode([ref[at] + m for at, m in zip(spans(GX, height(u), r), more)], planes, rows)

        by_rows(height(u) // GX, body)
        send_x(2, u, step)

    def own_sum(u):
        ref, raw, summed = chunk(u, 0), arrived_x(1, u), arrived_x(2, u)
        planes, came = (out_z.at[u], got_z.at[u]) if u < last else (tout_z, tgot_z)
        recv(raw, xrecv.at[1, u])
        recv(summed, xrecv.at[2, u])

        def body(r):
            rows = pl.ds(r, 16)
            one, two = decode(GX, raw, rows), decode(GX, summed, rows)
            for at, m, n in zip(spans(GX, height(u), r), one, two):
                ref[at] = ref[at] + m + n

        by_rows(height(u) // GX, body)
        given = ref.at[pl.ds(pl.multiple_of((1 - h) * ROWS, ROWS), ROWS)] if u < last else ref

        def body_z(r):
            encode([given[at] for at in spans(GZ, ROWS, r)], planes, pl.ds(r, 16))

        by_rows(ROWS // GZ, body_z)
        started.append(remote(planes, came, zsend.at[u], zrecv.at[u], dev(dh=1)))

    def finish(u):
        came = got_z.at[u] if u < last else tgot_z
        dst = gsum.at[lax.rem(y + offs[u // 2], NY), u % 2] if u < last else tsum
        kept = chunk(u, 0)
        if u < last:
            kept = kept.at[pl.ds(pl.multiple_of(h * ROWS, ROWS), ROWS)]
        recv(came, zrecv.at[u])

        def body(r):
            for at, m in zip(spans(GZ, ROWS, r), decode(GZ, came, pl.ds(r, 16))):
                dst[at] = kept[at] + m

        by_rows(ROWS // GZ, body)

    def half_block(t, i, tokens):
        return feats.at[lax.rem(y + offs[t], NY), HALVES[i], tokens]

    def to_sibling(t, i):
        ref = half_block(t, i, mine)
        started.append(remote(ref, ref, csend.at[t, i], crecv.at[t, i], dev(dc=1)))

    def neighbours(i):
        recv(half_block(1, i, mine), yrecv.at[1, i])
        recv(half_block(2, i, mine), yrecv.at[2, i])
        on = feats.at[lax.rem(y - step + NY, NY), HALVES[i], mine]
        started.append(remote(on, on, ysend.at[2, i], yrecv.at[3, i], dev(dy=step)))
        to_sibling(1, i)
        to_sibling(2, i)

    def opposite(i):
        recv(half_block(3, i, mine), yrecv.at[3, i])
        to_sibling(3, i)

    def compute(t, i):
        recv(half_block(t, i, other), crecv.at[t, i])
        product(2 * t + i)

    def tail():
        tailf[...] = jnp.zeros_like(tailf)
        for b in range(NY):
            tailf[0, 16 * b:16 * (b + 1)] = feats[b, WIDE:HELD]
            tailf[1, 64 + 16 * b:64 + 16 * (b + 1)] = feats[b, WIDE:HELD]
        product(last)

    compute(0, 0)
    compute(0, 1)
    forward_sum(0)
    neighbours(0)
    compute(1, 0)
    compute(2, 0)
    forward_sum(1)
    own_sum(0)
    neighbours(1)
    compute(1, 1)
    compute(2, 1)
    forward_sum(2)
    opposite(0)
    compute(3, 0)
    own_sum(1)
    forward_sum(4)
    opposite(1)
    compute(3, 1)
    tail()
    forward_sum(3)
    own_sum(2)
    forward_sum(5)
    finish(0)
    own_sum(4)
    forward_sum(6)
    finish(1)
    own_sum(3)
    forward_sum(7)
    forward_sum(8)
    own_sum(5)
    finish(2)
    own_sum(6)
    finish(4)
    finish(3)
    own_sum(7)
    own_sum(8)
    finish(5)
    finish(6)
    finish(7)
    finish(8)

    decay = 1.0 - STEP ** (-DECAY_POWER)
    ends = jnp.where(h == 0, tsum[:, 0:64], tsum[:, 64:128])
    for b in range(NY):
        for i in range(2):
            nat[:, BLOCK * b + UNIT * i:BLOCK * b + UNIT * (i + 1)] = gsum[b, i]
        nat[:, BLOCK * b + WIDE:BLOCK * (b + 1)] = ends[:, 16 * b:16 * b + REST]
    squares = nat[...] * nat[...]
    row_mean = jnp.sum(squares + EPS_GRAD, axis=1, keepdims=True) / D
    eye = (lax.broadcasted_iota(jnp.int32, (ROWS, ROWS), 0)
           == lax.broadcasted_iota(jnp.int32, (ROWS, ROWS), 1))
    row_old = jnp.sum(jnp.where(eye, row_ref[...], 0.0), axis=1, keepdims=True)
    row_stat = decay * row_old + (1.0 - decay) * row_mean
    row_out[...] = jnp.sum(jnp.where(eye, row_stat, 0.0), axis=0, keepdims=True)
    slot_a = x * NC + c
    slot_b = y * NH + h
    stat_a[slot_a, 0:1] = jnp.sum(squares + EPS_GRAD, axis=0, keepdims=True)
    stat_a[slot_a, 1:2] = jnp.sum(squares / row_stat, axis=0, keepdims=True)
    for i, (dx, dc) in enumerate(group_a):
        started.append(remote(stat_a.at[slot_a], stat_a.at[slot_a], ssend.at[0, i], srecv.at[0, i],
                              dev(dx=dx, dc=dc)))
    for i, (dx, dc) in enumerate(group_a):
        recv(stat_a.at[lax.rem(x - dx + NX, NX) * NC + lax.rem(c + dc, NC)], srecv.at[0, i])
    stat_b[slot_b] = jnp.sum(stat_a[...], axis=0)
    for i, (dy, dh) in enumerate(group_b):
        started.append(remote(stat_b.at[slot_b], stat_b.at[slot_b], ssend.at[1, i], srecv.at[1, i],
                              dev(dy=dy, dh=dh)))
    for i, (dy, dh) in enumerate(group_b):
        recv(stat_b.at[lax.rem(y - dy + NY, NY) * NH + lax.rem(h + dh, NH)], srecv.at[1, i])
    sums = jnp.sum(stat_b[...], axis=0)
    load_m.wait()
    col_stat = decay * col_ref[...] + (1.0 - decay) * (sums[0:1] / FF)
    col_out[...] = col_stat
    update_rms = jnp.sqrt(jnp.sum(sums[1:2] / col_stat, axis=1, keepdims=True) / (FF * D))
    scale = 1.0 / jnp.maximum(1.0, update_rms)
    direction = nat[...] * lax.rsqrt(row_stat) * (lax.rsqrt(col_stat) * scale)
    dir_ref[...] = direction
    master_new = held_m[...] - LEARNING_RATE * direction
    new_ref[...] = master_new
    plain[...] = master_new[:, 0:2 * HALF].astype(BF16)
    nat[...] = master_new
    padded = jnp.concatenate([nat[:, 2 * HALF:D], jnp.zeros((ROWS, 128 - OVER), F32)], axis=1)
    plain_e[...] = jnp.zeros_like(plain_e)
    plain_e[:, 0:ROWS] = padded.T[0:OVER, :].astype(BF16)
    rows_e[x, h, c] = plain_e[...]

    rows_in[x, h, c] = plain[:, pl.ds(pl.multiple_of(c * HALF, HALF), HALF)]

    def whole(body):
        @pl.loop(0, PARTS - 1)
        def _(p):
            body(p, PART)

    def rest(body):
        @pl.when(c == 1)
        def _():
            body(PARTS - 1, EXTRA)

    def start_of(p):
        return PART * p if isinstance(p, int) else pl.multiple_of(p * PART, PART)

    def piece(dx, dh, p, width):
        if width == EXTRA:
            return rows_e.at[lax.rem(x + dx + NX, NX), lax.rem(h + dh, NH)]
        return rows_in.at[lax.rem(x + dx + NX, NX), lax.rem(h + dh, NH), :, :, pl.ds(start_of(p), width)]

    def region(dx, p, core, width):
        size = width if width == PART else D - 2 * HALF
        return params_ref.at[
            pl.ds(pl.multiple_of(core * HALF + p * PART, 256 if width == PART else 1024), size),
            pl.ds(pl.multiple_of(lax.rem(x + dx + NX, NX) * 384, 384), 384)]

    def give(ref, kind, p, to):
        pltpu.make_async_remote_copy(
            src_ref=ref, dst_ref=ref, send_sem=gsend.at[kind, p], recv_sem=grecv.at[kind, p],
            device_id=to, device_id_type=MESH).start()

    def got(ref, kind, p):
        recv(ref, grecv.at[kind, p])

    def given(ref, kind, p):
        pltpu.make_async_remote_copy(
            src_ref=ref, dst_ref=ref, send_sem=gsend.at[kind, p], recv_sem=grecv.at[kind, p],
            device_id=dev(dc=1), device_id_type=MESH).wait_send()

    def turn(i, dx, p, width):
        ref = region(dx, p, c, width)
        if width == EXTRA:
            for q in range(NH * NC):
                wide_e[:, ROWS * q:ROWS * (q + 1)] = rows_e[
                    lax.rem(x + dx + NX, NX), q // NC, q % NC][:, 0:ROWS].astype(F32)
            ref[...] = wide_e[...].astype(BF16)
        for j in range(0, width if width == PART else 0, 128):
            at = pl.multiple_of(j + start_of(p), 128)
            value = rows_in[lax.rem(x + dx + NX, NX), :, :, :, pl.ds(at, 128)].reshape(NH * NC * ROWS, 128).T
            ref[j:j + 128, :] = value
        give(ref, 7 + i, p, dev(dc=1))

    ways = [(kind, k, to) for kind, to in enumerate((dict(dh=1), dict(dx=1), dict(dx=-1), dict()))
            for k in range(2) if (to or k)]

    def own_rows(p, width, kind, k, to):
        core = c if k == 0 else 1 - c
        if width == EXTRA:
            src, dst = plain_e, rows_e.at[x, h, c]
        else:
            src = plain.at[:, pl.ds(pl.multiple_of(core * HALF + start_of(p), 128), width)]
            dst = rows_in.at[x, h, c, :, pl.ds(start_of(p), width)]
        return pltpu.make_async_remote_copy(
            src_ref=src, dst_ref=dst,
            send_sem=osend.at[kind, k, p], recv_sem=orecv.at[kind, c, p],
            device_id=dev(dc=k, **to), device_id_type=MESH)

    def got_own(p, width, kind, dx, dh, owner):
        at = (lax.rem(x + dx + NX, NX), lax.rem(h + dh, NH), owner)
        ref = rows_e.at[at] if width == EXTRA else rows_in.at[(*at, slice(None), pl.ds(start_of(p), width))]
        recv(ref, orecv.at[kind, owner, p])

    def begin(p, width):
        for kind, k, to in ways:
            own_rows(p, width, kind, k, to).start()

    def begun(p, width):
        for kind, k, to in ways:
            own_rows(p, width, kind, k, to).wait_send()

    def middle(p, width):
        for owner in range(NC):
            got_own(p, width, 0, 0, 1, owner)
        ref = piece(0, 1, p, width)
        give(ref, 2, p, dev(dx=1))
        give(ref, 4, p, dev(dx=-1))
        for owner in range(NC):
            got_own(p, width, 1, -1, 0, owner)
            got_own(p, width, 2, 1, 0, owner)
        give(piece(-step, 0, p, width), 5, p, dev(dx=step))
        got_own(p, width, 3, 0, 0, 1 - c)
        turn(0, 0, p, width)

    def late(p, width):
        got(piece(-1, 1, p, width), 2, p)
        got(piece(1, 1, p, width), 4, p)

        def along_x():
            give(piece(-step, 1, p, width), 6, p, dev(dx=step))

        if width == PART:
            pl.when(p >= MIXED)(along_x)
        else:
            along_x()
        turn(1, 1, p, width)
        turn(2, -1, p, width)

    def final(p, width):
        def across():
            got(piece(2, 0, p, width), 5, p)

        if width == PART:
            pl.when(p >= MIXED)(across)
        else:
            across()
        got(piece(2, 1, p, width), 6, p)
        turn(3, 2, p, width)

    def shared(p, width):
        for i, dx in enumerate((0, 1, -1, 2)):
            got(region(dx, p, 1 - c, width), 7 + i, p)

    def sent(p, width):
        for kind, dx, dh in ((2, 0, 1), (4, 0, 1), (5, -step, 0), (6, -step, 1)):
            given(piece(dx, dh, p, width), kind, p)
        for i, dx in enumerate((0, 1, -1, 2)):
            given(region(dx, p, c, width), 7 + i, p)

    def extra_begin(body):
        for k in range(2):
            @pl.when(c == 1 - k)
            def _():
                for kind, k_, to in ways:
                    if k_ == k:
                        body(own_rows(PARTS - 1, EXTRA, kind, k, to))

    extra_begin(lambda copy: copy.start())
    whole(begin)
    rest(middle)
    whole(middle)
    for p in range(MIXED):
        got(piece(2, 0, p, PART), 5, p)
        give(piece(2, 0, p, PART), 6, p, dev(dh=1))
    for body in (late, final):
        rest(body)
        whole(body)
    whole(shared)
    pl.when(c == 0)(lambda: shared(PARTS - 1, EXTRA))
    whole(sent)
    rest(sent)
    whole(begun)
    extra_begin(lambda copy: copy.wait_send())
    for copy in started:
        copy.wait_send()


def write(*refs):
    sem = refs[-1]
    copies = [pltpu.make_async_copy(refs[i], refs[i + 5], sem.at[i]) for i in range(5)]
    for copy in copies:
        copy.start()
    for copy in copies:
        copy.wait()


def local(hidden, out_grad, master, row_prev, col_prev):
    vmem = pl.BlockSpec(memory_space=pltpu.VMEM)
    anywhere = pl.BlockSpec(memory_space=pl.ANY)
    dma = pltpu.SemaphoreType.DMA
    results = pl.pallas_call(
        kernel,
        out_shape=(
            pltpu.VMEM((D, NC * SLOTS * ROWS), BF16),
            pltpu.VMEM((ROWS, D), F32),
            pltpu.VMEM((ROWS, D), F32),
            pltpu.VMEM((1, ROWS), F32),
            pltpu.VMEM((1, D), F32),
        ),
        in_specs=[anywhere, anywhere, anywhere, vmem, vmem],
        out_specs=(vmem, vmem, vmem, vmem, vmem),
        scratch_shapes=[
            pltpu.VMEM((TOK, NC * SLOTS * ROWS), BF16),
            pltpu.VMEM((BLOCK, TOK), BF16),
            pltpu.VMEM((SLOTS, NC, ROWS, TOK), BF16),
            pltpu.VMEM((SLOTS, ROWS, NC * TOK), BF16),
            pltpu.VMEM((NY, HELD, NC * TOK), BF16),
            pltpu.VMEM((NH, TAIL, NC * TOK), BF16),
            pltpu.VMEM((UNITS, NX, PAIR, UNIT), F32),
            pltpu.VMEM((NX, ROWS, TAIL), F32),
            pltpu.VMEM((3, UNITS, GX + 1, PAIR // GX, UNIT), BF16),
            pltpu.VMEM((UNITS, GZ + 1, ROWS // GZ, UNIT), BF16),
            pltpu.VMEM((3, GX + 1, ROWS // GX, TAIL), BF16),
            pltpu.VMEM((GZ + 1, ROWS // GZ, TAIL), BF16),
            pltpu.VMEM((3, UNITS, GX + 1, PAIR // GX, UNIT), BF16),
            pltpu.VMEM((UNITS, GZ + 1, ROWS // GZ, UNIT), BF16),
            pltpu.VMEM((3, GX + 1, ROWS // GX, TAIL), BF16),
            pltpu.VMEM((GZ + 1, ROWS // GZ, TAIL), BF16),
            pltpu.VMEM((NY, 2, ROWS, UNIT), F32),
            pltpu.VMEM((ROWS, TAIL), F32),
            pltpu.VMEM((ROWS, D), F32),
            pltpu.VMEM((ROWS, D), F32),
            pltpu.VMEM((NX * NC, 2, D), F32),
            pltpu.VMEM((NY * NH, 2, D), F32),
            pltpu.VMEM((ROWS, HALF * 2), BF16),
            pltpu.VMEM((NX, NH, NC, ROWS, HALF), BF16),
            pltpu.VMEM((OVER, 128), BF16),
            pltpu.VMEM((NX, NH, NC, OVER, 128), BF16),
            pltpu.VMEM((OVER, NH * NC * ROWS), F32),
            dma((3,)), dma,
            dma((3, 2)), dma((4, 2)), dma((4, 2)), dma((4, 2)), dma((1,)), dma((1,)),
            dma((3, UNITS + 1)), dma((3, UNITS + 1)), dma((UNITS + 1,)), dma((UNITS + 1,)),
            dma((2, 7)), dma((2, 7)),
            dma((11, PARTS)), dma((11, PARTS)), dma((4, 2, PARTS)), dma((4, 2, PARTS)),
        ],
        compiler_params=pltpu.CompilerParams(
            collective_id=0, has_side_effects=True, vmem_limit_bytes=50 * 2**20),
        cost_estimate=pl.CostEstimate(
            flops=2 * TOK * FF // NY * D, bytes_accessed=16 * 2**20, transcendentals=0),
        name="factored_step",
    )(hidden[0], out_grad[0].T, master[0], row_prev, col_prev)
    params, master_new, direction, row_stat, col_stat = pl.pallas_call(
        write,
        out_shape=[pltpu.HBM(r.shape, r.dtype) for r in results],
        in_specs=[vmem] * 5,
        out_specs=[pl.BlockSpec(memory_space=pltpu.HBM)] * 5,
        scratch_shapes=[dma((5,))],
        compiler_params=pltpu.CompilerParams(vmem_limit_bytes=2 * 2**20),
        name="write_results",
    )(*[pltpu.with_memory_space_constraint(r, pltpu.VMEM) for r in results])
    return params.T[None], master_new[None], direction[None], row_stat, col_stat


def solution(mesh):
    in_specs = (
        P("expert", "dp", "mp"),
        P("expert", "dp", "mp"),
        P("expert", ("mp", "dp"), None),
        P("expert", ("mp", "dp")),
        P("expert", None),
    )
    out_specs = (
        P("expert", "mp", None),
        P("expert", ("mp", "dp"), None),
        P("expert", ("mp", "dp"), None),
        P("expert", ("mp", "dp")),
        P("expert", None),
    )
    return jax.shard_map(local, mesh=mesh, in_specs=in_specs, out_specs=out_specs, check_vma=False)
```

```python
import functools

import jax
import jax.numpy as jnp
from jax import lax
from jax.experimental import pallas as pl
from jax.experimental.pallas import tpu as pltpu
from jax.sharding import PartitionSpec as P

D = 2080
FF = 6144
STEP = 100
DECAY_POWER = 0.8
EPS_GRAD = 1e-30
LEARNING_RATE = 0.01

NX, NH, NC, NY = 4, 2, 2, 4
TOK = 512
ROWS = 96
SLOTS = NX * NH
WIDE = 512
BLOCK = D // NY
REST = BLOCK - WIDE
HELD = WIDE + 16
TAIL = 128
HALF = 1024
PART = 256
EXTRA = 128
OVER = D - 2 * HALF
PARTS = 5
MIXED = 1
MESH = pl.DeviceIdType.MESH
F32 = jnp.float32
BF16 = jnp.bfloat16

UNIT = 256
UNITS = NY * WIDE // UNIT

LEVELS = 21
REACH = 10.4 * 256
TINY = 1e-30


def last_place(wide):
    x = jnp.abs(wide) * 0.7515
    big = x * (2.0 ** 23 + 1.0)
    return big + (x - big)


def split(value, groups):
    high = value.astype(BF16)
    wide = high.astype(F32)
    if groups == 2:
        inverse = pl.reciprocal(jnp.maximum(jnp.abs(wide), TINY), approx=True)
        return high, jnp.round((value - wide) * (inverse * REACH))
    inverse = pl.reciprocal(jnp.maximum(last_place(wide), TINY), approx=True)
    step = jnp.floor((value - wide) * (inverse * 1024.0))
    return high, jnp.minimum(jnp.maximum(step, -4.0), 3.0)


def encode(values, planes, rows):
    groups = len(values)
    steps = []
    for i, value in enumerate(values):
        high, step = split(value, groups)
        planes[i, rows] = high
        steps.append(step)
    if groups == 2:
        low = steps[0] * LEVELS + steps[1]
    else:
        low = steps[0] * 64.0 + (steps[1] * 8.0 + (steps[2] + 36.0))
    planes[groups, rows] = low.astype(BF16)


def decode(groups, planes, rows):
    low = planes[groups, rows].astype(F32)
    wides = [planes[i, rows].astype(F32) for i in range(groups)]
    if groups == 2:
        step_1 = jnp.round(low * (1.0 / LEVELS))
        steps = (step_1, low - LEVELS * step_1)
        return [w + jnp.abs(w) * (q * (1.0 / REACH)) for w, q in zip(wides, steps)]
    step_1 = jnp.floor(low * (1.0 / 64))
    low = low - 64.0 * step_1
    step_2 = jnp.floor(low * (1.0 / 8))
    step_3 = low - 8.0 * step_2
    shifted = (step_1 + 0.5, step_2 - 3.5, step_3 - 3.5)
    return [w + last_place(w) * (q * (1.0 / 1024)) for w, q in zip(wides, shifted)]


GX, GZ = 3, 3
HALVES = (pl.ds(0, UNIT), pl.ds(UNIT, HELD - UNIT))
PAIR = NH * ROWS


def by_rows(count, body):
    @pl.loop(0, count // 16)
    def _(i):
        body(pl.multiple_of(i * 16, 16))


def kernel(hidden_ref, grad_ref, master_ref, row_ref, col_ref,
           params_ref, new_ref, dir_ref, row_out, col_out,
           hid, own_grad, turned, lhs, feats, tailf, wide_p, tail_p,
           out_x, out_z, tout_x, tout_z,
           got_x, got_z, tgot_x, tgot_z,
           gsum, tsum, nat, held_m, stat_a, stat_b, plain, rows_in, plain_e, rows_e, wide_e,
           load_sem, copy_sem,
           ysend, yrecv, csend, crecv, hsend, hrecv,
           xsend, xrecv, zsend, zrecv, ssend, srecv,
           gsend, grecv, osend, orecv):
    dp, ex, y = lax.axis_index("dp"), lax.axis_index("expert"), lax.axis_index("mp")
    x, h, c = dp // 4, lax.rem(dp // 2, 2), lax.rem(dp, 2)
    step = 1 - 2 * c

    def dev(dx=0, dh=0, dc=0, dy=0):
        return (
            (lax.rem(x + dx + NX, NX) * NH + lax.rem(h + dh, NH)) * NC + lax.rem(c + dc, NC),
            ex,
            lax.rem(y + dy + NY, NY),
        )

    def remote(src, dst, send, recv, to):
        copy = pltpu.make_async_remote_copy(
            src_ref=src, dst_ref=dst, send_sem=send, recv_sem=recv,
            device_id=to, device_id_type=MESH)
        copy.start()
        return copy

    started = []

    load_h = pltpu.make_async_copy(hidden_ref, hid, load_sem.at[0])
    load_h.start()
    mine = pl.ds(pl.multiple_of(c * TOK, TOK), TOK)
    other = pl.ds(pl.multiple_of((1 - c) * TOK, TOK), TOK)
    load_g = pltpu.make_async_copy(grad_ref, own_grad, load_sem.at[1])
    load_g.start()
    load_m = pltpu.make_async_copy(master_ref, held_m, load_sem.at[2])
    load_m.start()

    group_a = [(dx, dc) for dx in range(NX) for dc in range(NC) if (dx, dc) != (0, 0)]
    group_b = [(dy, dh) for dy in range(NY) for dh in range(NH) if (dy, dh) != (0, 0)]
    barrier = pltpu.get_barrier_semaphore()
    for dx, dc in group_a:
        pl.semaphore_signal(barrier, 1, device_id=dev(dx=dx, dc=dc), device_id_type=MESH)
    for dy, dh in group_b:
        pl.semaphore_signal(barrier, 1, device_id=dev(dy=dy, dh=dh), device_id_type=MESH)

    load_h.wait()
    for g in range(4):
        part = hid[:, pl.ds(384 * g, 384)].T
        for q in range(4):
            turned[2 * g + q // 2, q % 2] = part[ROWS * q:ROWS * (q + 1), :]
    load_g.wait()
    feats[y, 0:WIDE, mine] = own_grad[0:WIDE, :]
    feats[y, WIDE:HELD, mine] = jnp.concatenate(
        [own_grad[WIDE:BLOCK, :], jnp.zeros((HELD - BLOCK, TOK), BF16)], axis=0)
    pl.semaphore_wait(barrier, len(group_a) + len(group_b))

    give_h = remote(turned.at[:, 1 - c], lhs.at[:, :, mine], hsend.at[0], hrecv.at[0], dev(dc=1))
    keep_h = pltpu.make_async_copy(turned.at[:, c], lhs.at[:, :, mine], copy_sem)
    keep_h.start()
    for i in range(2):
        own_i = feats.at[y, HALVES[i], mine]
        started.append(remote(own_i, own_i, csend.at[0, i], crecv.at[0, i], dev(dc=1)))
        started.append(remote(own_i, own_i, ysend.at[0, i], yrecv.at[2, i], dev(dy=1)))
        started.append(remote(own_i, own_i, ysend.at[1, i], yrecv.at[1, i], dev(dy=-1)))
    keep_h.wait()
    give_h.wait()

    offs = (0, 1, 3, 2)
    last = UNITS

    def sent_x(kind, u):
        return out_x.at[kind, u] if u < last else tout_x.at[kind]

    def arrived_x(kind, u):
        return got_x.at[kind, u] if u < last else tgot_x.at[kind]

    def chunk(u, dx):
        return (wide_p.at[u] if u < last else tail_p).at[lax.rem(x + dx + NX, NX)]

    def height(u):
        return PAIR if u < last else ROWS

    def times(left, right):
        return lax.dot_general(left, right, (((1,), (1,)), ((), ())), preferred_element_type=F32)

    def send_x(kind, u, dx):
        started.append(remote(sent_x(kind, u), arrived_x(kind, u),
                              xsend.at[kind, u], xrecv.at[kind, u], dev(dx=dx)))

    def spans(groups, total, r):
        return [pl.ds(i * (total // groups) + r, 16) for i in range(groups)]

    def send_raw(kind, u, of, dx):
        ref, planes = chunk(u, of), sent_x(kind, u)

        def body(r):
            encode([ref[rows] for rows in spans(GX, height(u), r)], planes, pl.ds(r, 16))

        by_rows(height(u) // GX, body)
        send_x(kind, u, dx)

    def product(u):
        if u < last:
            block, first = lax.rem(y + offs[u // 2], NY), UNIT * (u % 2)

        @pl.loop(0, NX // 2)
        def _(i):
            if u < last:
                left = lhs[pl.ds(4 * i, 4)].reshape(2 * PAIR, 2 * TOK)
                wide_p[u, pl.ds(2 * i, 2)] = times(
                    left, feats[block, first:first + UNIT, :]).reshape(2, PAIR, UNIT)
            else:
                for j in range(2):
                    at = 2 * i + j
                    tail_p[at] = times(lhs[2 * at], tailf[0]) + times(lhs[2 * at + 1], tailf[1])

        send_raw(0, u, 2, step)
        send_raw(1, u, -step, -step)

    def recv(dst, sem):
        pltpu.make_async_remote_copy(
            src_ref=dst, dst_ref=dst, send_sem=sem, recv_sem=sem,
            device_id=dev(dc=1), device_id_type=MESH).wait_recv()

    def forward_sum(u):
        came, ref, planes = arrived_x(0, u), chunk(u, step), sent_x(2, u)
        recv(came, xrecv.at[0, u])

        def body(r):
            rows = pl.ds(r, 16)
            more = decode(GX, came, rows)
            encode([ref[at] + m for at, m in zip(spans(GX, height(u), r), more)], planes, rows)

        by_rows(height(u) // GX, body)
        send_x(2, u, step)

    def own_sum(u):
        ref, raw, summed = chunk(u, 0), arrived_x(1, u), arrived_x(2, u)
        planes, came = (out_z.at[u], got_z.at[u]) if u < last else (tout_z, tgot_z)
        recv(raw, xrecv.at[1, u])
        recv(summed, xrecv.at[2, u])

        def body(r):
            rows = pl.ds(r, 16)
            one, two = decode(GX, raw, rows), decode(GX, summed, rows)
            for at, m, n in zip(spans(GX, height(u), r), one, two):
                ref[at] = ref[at] + m + n

        by_rows(height(u) // GX, body)
        given = ref.at[pl.ds(pl.multiple_of((1 - h) * ROWS, ROWS), ROWS)] if u < last else ref

        def body_z(r):
            encode([given[at] for at in spans(GZ, ROWS, r)], planes, pl.ds(r, 16))

        by_rows(ROWS // GZ, body_z)
        started.append(remote(planes, came, zsend.at[u], zrecv.at[u], dev(dh=1)))

    def finish(u):
        came = got_z.at[u] if u < last else tgot_z
        dst = gsum.at[lax.rem(y + offs[u // 2], NY), u % 2] if u < last else tsum
        kept = chunk(u, 0)
        if u < last:
            kept = kept.at[pl.ds(pl.multiple_of(h * ROWS, ROWS), ROWS)]
        recv(came, zrecv.at[u])

        def body(r):
            for at, m in zip(spans(GZ, ROWS, r), decode(GZ, came, pl.ds(r, 16))):
                dst[at] = kept[at] + m

        by_rows(ROWS // GZ, body)

    def half_block(t, i, tokens):
        return feats.at[lax.rem(y + offs[t], NY), HALVES[i], tokens]

    def to_sibling(t, i):
        ref = half_block(t, i, mine)
        started.append(remote(ref, ref, csend.at[t, i], crecv.at[t, i], dev(dc=1)))

    def neighbours(i):
        recv(half_block(1, i, mine), yrecv.at[1, i])
        recv(half_block(2, i, mine), yrecv.at[2, i])
        on = feats.at[lax.rem(y - step + NY, NY), HALVES[i], mine]
        started.append(remote(on, on, ysend.at[2, i], yrecv.at[3, i], dev(dy=step)))
        to_sibling(1, i)
        to_sibling(2, i)

    def opposite(i):
        recv(half_block(3, i, mine), yrecv.at[3, i])
        to_sibling(3, i)

    def compute(t, i):
        recv(half_block(t, i, other), crecv.at[t, i])
        product(2 * t + i)

    def tail():
        tailf[...] = jnp.zeros_like(tailf)
        for b in range(NY):
            tailf[0, 16 * b:16 * (b + 1)] = feats[b, WIDE:HELD]
            tailf[1, 64 + 16 * b:64 + 16 * (b + 1)] = feats[b, WIDE:HELD]
        product(last)

    compute(0, 0)
    compute(0, 1)
    forward_sum(0)
    neighbours(0)
    compute(1, 0)
    compute(2, 0)
    forward_sum(1)
    own_sum(0)
    neighbours(1)
    compute(1, 1)
    compute(2, 1)
    forward_sum(2)
    opposite(0)
    compute(3, 0)
    own_sum(1)
    forward_sum(4)
    opposite(1)
    compute(3, 1)
    tail()
    forward_sum(3)
    own_sum(2)
    forward_sum(5)
    finish(0)
    own_sum(4)
    forward_sum(6)
    finish(1)
    own_sum(3)
    forward_sum(7)
    forward_sum(8)
    own_sum(5)
    finish(2)
    own_sum(6)
    finish(4)
    finish(3)
    own_sum(7)
    own_sum(8)
    finish(5)
    finish(6)
    finish(7)
    finish(8)

    decay = 1.0 - STEP ** (-DECAY_POWER)
    ends = jnp.where(h == 0, tsum[:, 0:64], tsum[:, 64:128])
    for b in range(NY):
        for i in range(2):
            nat[:, BLOCK * b + UNIT * i:BLOCK * b + UNIT * (i + 1)] = gsum[b, i]
        nat[:, BLOCK * b + WIDE:BLOCK * (b + 1)] = ends[:, 16 * b:16 * b + REST]
    squares = nat[...] * nat[...]
    row_mean = jnp.sum(squares + EPS_GRAD, axis=1, keepdims=True) / D
    eye = (lax.broadcasted_iota(jnp.int32, (ROWS, ROWS), 0)
           == lax.broadcasted_iota(jnp.int32, (ROWS, ROWS), 1))
    row_old = jnp.sum(jnp.where(eye, row_ref[...], 0.0), axis=1, keepdims=True)
    row_stat = decay * row_old + (1.0 - decay) * row_mean
    row_out[...] = jnp.sum(jnp.where(eye, row_stat, 0.0), axis=0, keepdims=True)
    slot_a = x * NC + c
    slot_b = y * NH + h
    stat_a[slot_a, 0:1] = jnp.sum(squares + EPS_GRAD, axis=0, keepdims=True)
    stat_a[slot_a, 1:2] = jnp.sum(squares / row_stat, axis=0, keepdims=True)
    for i, (dx, dc) in enumerate(group_a):
        started.append(remote(stat_a.at[slot_a], stat_a.at[slot_a], ssend.at[0, i], srecv.at[0, i],
                              dev(dx=dx, dc=dc)))
    for i, (dx, dc) in enumerate(group_a):
        recv(stat_a.at[lax.rem(x - dx + NX, NX) * NC + lax.rem(c + dc, NC)], srecv.at[0, i])
    stat_b[slot_b] = jnp.sum(stat_a[...], axis=0)
    for i, (dy, dh) in enumerate(group_b):
        started.append(remote(stat_b.at[slot_b], stat_b.at[slot_b], ssend.at[1, i], srecv.at[1, i],
                              dev(dy=dy, dh=dh)))
    for i, (dy, dh) in enumerate(group_b):
        recv(stat_b.at[lax.rem(y - dy + NY, NY) * NH + lax.rem(h + dh, NH)], srecv.at[1, i])
    sums = jnp.sum(stat_b[...], axis=0)
    load_m.wait()
    col_stat = decay * col_ref[...] + (1.0 - decay) * (sums[0:1] / FF)
    col_out[...] = col_stat
    update_rms = jnp.sqrt(jnp.sum(sums[1:2] / col_stat, axis=1, keepdims=True) / (FF * D))
    scale = 1.0 / jnp.maximum(1.0, update_rms)
    direction = nat[...] * lax.rsqrt(row_stat) * (lax.rsqrt(col_stat) * scale)
    dir_ref[...] = direction
    master_new = held_m[...] - LEARNING_RATE * direction
    new_ref[...] = master_new
    plain[...] = master_new[:, 0:2 * HALF].astype(BF16)
    nat[...] = master_new
    padded = jnp.concatenate([nat[:, 2 * HALF:D], jnp.zeros((ROWS, 128 - OVER), F32)], axis=1)
    plain_e[...] = jnp.zeros_like(plain_e)
    plain_e[:, 0:ROWS] = padded.T[0:OVER, :].astype(BF16)
    rows_e[x, h, c] = plain_e[...]

    rows_in[x, h, c] = plain[:, pl.ds(pl.multiple_of(c * HALF, HALF), HALF)]

    def whole(body):
        @pl.loop(0, PARTS - 1)
        def _(p):
            body(p, PART)

    def rest(body):
        @pl.when(c == 1)
        def _():
            body(PARTS - 1, EXTRA)

    def start_of(p):
        return PART * p if isinstance(p, int) else pl.multiple_of(p * PART, PART)

    def piece(dx, dh, p, width):
        if width == EXTRA:
            return rows_e.at[lax.rem(x + dx + NX, NX), lax.rem(h + dh, NH)]
        return rows_in.at[lax.rem(x + dx + NX, NX), lax.rem(h + dh, NH), :, :, pl.ds(start_of(p), width)]

    def region(dx, p, core, width):
        size = width if width == PART else D - 2 * HALF
        return params_ref.at[
            pl.ds(pl.multiple_of(core * HALF + p * PART, 256 if width == PART else 1024), size),
            pl.ds(pl.multiple_of(lax.rem(x + dx + NX, NX) * 384, 384), 384)]

    def give(ref, kind, p, to):
        pltpu.make_async_remote_copy(
            src_ref=ref, dst_ref=ref, send_sem=gsend.at[kind, p], recv_sem=grecv.at[kind, p],
            device_id=to, device_id_type=MESH).start()

    def got(ref, kind, p):
        recv(ref, grecv.at[kind, p])

    def given(ref, kind, p):
        pltpu.make_async_remote_copy(
            src_ref=ref, dst_ref=ref, send_sem=gsend.at[kind, p], recv_sem=grecv.at[kind, p],
            device_id=dev(dc=1), device_id_type=MESH).wait_send()

    def turn(i, dx, p, width):
        ref = region(dx, p, c, width)
        if width == EXTRA:
            for q in range(NH * NC):
                wide_e[:, ROWS * q:ROWS * (q + 1)] = rows_e[
                    lax.rem(x + dx + NX, NX), q // NC, q % NC][:, 0:ROWS].astype(F32)
            ref[...] = wide_e[...].astype(BF16)
        for j in range(0, width if width == PART else 0, 128):
            at = pl.multiple_of(j + start_of(p), 128)
            value = rows_in[lax.rem(x + dx + NX, NX), :, :, :, pl.ds(at, 128)].reshape(NH * NC * ROWS, 128).T
            ref[j:j + 128, :] = value
        give(ref, 7 + i, p, dev(dc=1))

    ways = [(kind, k, to) for kind, to in enumerate((dict(dh=1), dict(dx=1), dict(dx=-1), dict()))
            for k in range(2) if (to or k)]

    def own_rows(p, width, kind, k, to):
        core = c if k == 0 else 1 - c
        if width == EXTRA:
            src, dst = plain_e, rows_e.at[x, h, c]
        else:
            src = plain.at[:, pl.ds(pl.multiple_of(core * HALF + start_of(p), 128), width)]
            dst = rows_in.at[x, h, c, :, pl.ds(start_of(p), width)]
        return pltpu.make_async_remote_copy(
            src_ref=src, dst_ref=dst,
            send_sem=osend.at[kind, k, p], recv_sem=orecv.at[kind, c, p],
            device_id=dev(dc=k, **to), device_id_type=MESH)

    def got_own(p, width, kind, dx, dh, owner):
        at = (lax.rem(x + dx + NX, NX), lax.rem(h + dh, NH), owner)
        ref = rows_e.at[at] if width == EXTRA else rows_in.at[(*at, slice(None), pl.ds(start_of(p), width))]
        recv(ref, orecv.at[kind, owner, p])

    def begin(p, width):
        for kind, k, to in ways:
            own_rows(p, width, kind, k, to).start()

    def begun(p, width):
        for kind, k, to in ways:
            own_rows(p, width, kind, k, to).wait_send()

    def middle(p, width):
        for owner in range(NC):
            got_own(p, width, 0, 0, 1, owner)
        ref = piece(0, 1, p, width)
        give(ref, 2, p, dev(dx=1))
        give(ref, 4, p, dev(dx=-1))
        for owner in range(NC):
            got_own(p, width, 1, -1, 0, owner)
            got_own(p, width, 2, 1, 0, owner)
        give(piece(-step, 0, p, width), 5, p, dev(dx=step))
        got_own(p, width, 3, 0, 0, 1 - c)
        turn(0, 0, p, width)

    def late(p, width):
        got(piece(-1, 1, p, width), 2, p)
        got(piece(1, 1, p, width), 4, p)

        def along_x():
            give(piece(-step, 1, p, width), 6, p, dev(dx=step))

        if width == PART:
            pl.when(p >= MIXED)(along_x)
        else:
            along_x()
        turn(1, 1, p, width)
        turn(2, -1, p, width)

    def final(p, width):
        def across():
            got(piece(2, 0, p, width), 5, p)

        if width == PART:
            pl.when(p >= MIXED)(across)
        else:
            across()
        got(piece(2, 1, p, width), 6, p)
        turn(3, 2, p, width)

    def shared(p, width):
        for i, dx in enumerate((0, 1, -1, 2)):
            got(region(dx, p, 1 - c, width), 7 + i, p)

    def sent(p, width):
        for kind, dx, dh in ((2, 0, 1), (4, 0, 1), (5, -step, 0), (6, -step, 1)):
            given(piece(dx, dh, p, width), kind, p)
        for i, dx in enumerate((0, 1, -1, 2)):
            given(region(dx, p, c, width), 7 + i, p)

    def extra_begin(body):
        for k in range(2):
            @pl.when(c == 1 - k)
            def _():
                for kind, k_, to in ways:
                    if k_ == k:
                        body(own_rows(PARTS - 1, EXTRA, kind, k, to))

    extra_begin(lambda copy: copy.start())
    whole(begin)
    rest(middle)
    whole(middle)
    for p in range(MIXED):
        got(piece(2, 0, p, PART), 5, p)
        give(piece(2, 0, p, PART), 6, p, dev(dh=1))
    for body in (late, final):
        rest(body)
        whole(body)
    whole(shared)
    pl.when(c == 0)(lambda: shared(PARTS - 1, EXTRA))
    whole(sent)
    rest(sent)
    whole(begun)
    extra_begin(lambda copy: copy.wait_send())
    for copy in started:
        copy.wait_send()


def write(*refs):
    sem = refs[-1]
    copies = [pltpu.make_async_copy(refs[i], refs[i + 5], sem.at[i]) for i in range(5)]
    for copy in copies:
        copy.start()
    for copy in copies:
        copy.wait()


def local(hidden, out_grad, master, row_prev, col_prev):
    vmem = pl.BlockSpec(memory_space=pltpu.VMEM)
    anywhere = pl.BlockSpec(memory_space=pl.ANY)
    dma = pltpu.SemaphoreType.DMA
    results = pl.pallas_call(
        kernel,
        out_shape=(
            pltpu.VMEM((D, NC * SLOTS * ROWS), BF16),
            pltpu.VMEM((ROWS, D), F32),
            pltpu.VMEM((ROWS, D), F32),
            pltpu.VMEM((1, ROWS), F32),
            pltpu.VMEM((1, D), F32),
        ),
        in_specs=[anywhere, anywhere, anywhere, vmem, vmem],
        out_specs=(vmem, vmem, vmem, vmem, vmem),
        scratch_shapes=[
            pltpu.VMEM((TOK, NC * SLOTS * ROWS), BF16),
            pltpu.VMEM((BLOCK, TOK), BF16),
            pltpu.VMEM((SLOTS, NC, ROWS, TOK), BF16),
            pltpu.VMEM((SLOTS, ROWS, NC * TOK), BF16),
            pltpu.VMEM((NY, HELD, NC * TOK), BF16),
            pltpu.VMEM((NH, TAIL, NC * TOK), BF16),
            pltpu.VMEM((UNITS, NX, PAIR, UNIT), F32),
            pltpu.VMEM((NX, ROWS, TAIL), F32),
            pltpu.VMEM((3, UNITS, GX + 1, PAIR // GX, UNIT), BF16),
            pltpu.VMEM((UNITS, GZ + 1, ROWS // GZ, UNIT), BF16),
            pltpu.VMEM((3, GX + 1, ROWS // GX, TAIL), BF16),
            pltpu.VMEM((GZ + 1, ROWS // GZ, TAIL), BF16),
            pltpu.VMEM((3, UNITS, GX + 1, PAIR // GX, UNIT), BF16),
            pltpu.VMEM((UNITS, GZ + 1, ROWS // GZ, UNIT), BF16),
            pltpu.VMEM((3, GX + 1, ROWS // GX, TAIL), BF16),
            pltpu.VMEM((GZ + 1, ROWS // GZ, TAIL), BF16),
            pltpu.VMEM((NY, 2, ROWS, UNIT), F32),
            pltpu.VMEM((ROWS, TAIL), F32),
            pltpu.VMEM((ROWS, D), F32),
            pltpu.VMEM((ROWS, D), F32),
            pltpu.VMEM((NX * NC, 2, D), F32),
            pltpu.VMEM((NY * NH, 2, D), F32),
            pltpu.VMEM((ROWS, HALF * 2), BF16),
            pltpu.VMEM((NX, NH, NC, ROWS, HALF), BF16),
            pltpu.VMEM((OVER, 128), BF16),
            pltpu.VMEM((NX, NH, NC, OVER, 128), BF16),
            pltpu.VMEM((OVER, NH * NC * ROWS), F32),
            dma((3,)), dma,
            dma((3, 2)), dma((4, 2)), dma((4, 2)), dma((4, 2)), dma((1,)), dma((1,)),
            dma((3, UNITS + 1)), dma((3, UNITS + 1)), dma((UNITS + 1,)), dma((UNITS + 1,)),
            dma((2, 7)), dma((2, 7)),
            dma((11, PARTS)), dma((11, PARTS)), dma((4, 2, PARTS)), dma((4, 2, PARTS)),
        ],
        compiler_params=pltpu.CompilerParams(
            collective_id=0, has_side_effects=True, vmem_limit_bytes=50 * 2**20),
        cost_estimate=pl.CostEstimate(
            flops=2 * TOK * FF // NY * D, bytes_accessed=16 * 2**20, transcendentals=0),
        name="factored_step",
    )(hidden[0], out_grad[0].T, master[0], row_prev, col_prev)
    params, master_new, direction, row_stat, col_stat = pl.pallas_call(
        write,
        out_shape=[pltpu.HBM(r.shape, r.dtype) for r in results],
        in_specs=[vmem] * 5,
        out_specs=[pl.BlockSpec(memory_space=pltpu.HBM)] * 5,
        scratch_shapes=[dma((5,))],
        compiler_params=pltpu.CompilerParams(vmem_limit_bytes=2 * 2**20),
        name="write_results",
    )(*[pltpu.with_memory_space_constraint(r, pltpu.VMEM) for r in results])
    return params.T[None], master_new[None], direction[None], row_stat, col_stat


def solution(mesh):
    in_specs = (
        P("expert", "dp", "mp"),
        P("expert", "dp", "mp"),
        P("expert", ("mp", "dp"), None),
        P("expert", ("mp", "dp")),
        P("expert", None),
    )
    out_specs = (
        P("expert", "mp", None),
        P("expert", ("mp", "dp"), None),
        P("expert", ("mp", "dp"), None),
        P("expert", ("mp", "dp")),
        P("expert", None),
    )
    return jax.shard_map(local, mesh=mesh, in_specs=in_specs, out_specs=out_specs, check_vma=False)
```
